256 devices in a mesh: layer: 32 (over y, z_lo, core), batch: 8 (over x, z_hi).
Axes of the slice: x: 4, y: 4, z: 8 (z_hi: 2, z_lo: 4; z = z_hi * 4 + z_lo), core: 2. Of those that a mesh axis runs over, the one named last changes fastest.
Arguments:
- u_c: bfloat16 [32, 64, 32, 32, 128], P('layer', 'batch'), may hold values from -6 to 6
- lam_c: bfloat16 [32, 64, 32, 32, 128], P('layer', 'batch'), may hold values from -6 to 6
- weights: bfloat16 [64, 3, 3, 128, 128], P('layer'), may hold values from -0.1875 to 0.1875
Outputs:
- lam_low: bfloat16 [32, 64, 32, 32, 128], P('layer', 'batch')
- weight_grad: float32 [64, 3, 3, 128, 128], P('layer')
The draws below stay inside these ranges and needn't reach their ends.
All inputs are finite; a program needn't handle non-finite values.
Results may differ from the reference program's by a relative error of at most 0.02.
Values may be sent and summed in bfloat16 or wider, within the bound.
A program may use at most 64 MiB of HBM per device.

```python
import jax
import jax.numpy as jnp
from jax import lax

C = 128
H = 32
W = 32
STRIDE = 2
GROUPS = 32
LAYERS = 64
BATCH = 64
N_BATCH = 8


def block_scale(key, extent, split, low, top_value):
    gain = 1.0
    for position, shards_of in split:
        heights = jax.random.uniform(jax.random.fold_in(jax.random.fold_in(key, 6), position), (shards_of,), jnp.float32, low / len(split), top_value / len(split))
        gain = gain * jnp.repeat(jnp.exp(heights), extent[position] // shards_of).reshape((-1,) + (1,) * (len(extent) - 1 - position))
    return gain


def scatter_about(rng, shape, spread, most, cuts=(), held_as=jnp.bfloat16):
    result = jax.random.normal(rng, shape, jnp.float32) * spread
    if len(cuts) > 0:
        result = block_scale(rng, shape, cuts, -0.22, 0.18) * result
    return jnp.clip(result, min=-most, max=most).astype(held_as)


def setup_inputs(seed: int = 0) -> dict:
    streams_of = jax.random.split(jax.random.key(seed), 4)
    return {
        "u_c": scatter_about(streams_of[0], (GROUPS, BATCH, H, W, C), 1.0, 6.0, ((0, 32), (1, 8))),
        "lam_c": scatter_about(streams_of[1], (GROUPS, BATCH, H, W, C), 1.0, 6.0, ((0, 32), (1, 8))),
        "weights": scatter_about(streams_of[2], (LAYERS, 3, 3, C, C), (9 * C) ** -0.5, 0.1875, ((0, 32),)),
    }


depth_step = 0.5

def conv_apply(values, kernel):
    return lax.conv_general_dilated(values, kernel, (1, 1), 'SAME', dimension_numbers=('NHWC', 'HWIO', 'NHWC'), preferred_element_type=jnp.float32)

def conv_transpose(adjoint, kernel):
    flipped = jnp.transpose(kernel[::-1, ::-1], (0, 1, 3, 2))
    return conv_apply(adjoint, flipped)

def advance(activation, kernel):
    widened = activation.astype(jnp.float32)
    active = jax.nn.silu(widened).astype(jnp.bfloat16)
    return (widened + depth_step * conv_apply(active, kernel)).astype(jnp.bfloat16)

def retreat(adjoint, activation, kernel):
    pulled = conv_transpose(adjoint, kernel)
    widened = activation.astype(jnp.float32)
    sigmoid_value = jax.nn.sigmoid(widened)
    derivative = sigmoid_value * (1.0 + widened * (1.0 - sigmoid_value))
    return (adjoint.astype(jnp.float32) + depth_step * derivative * pulled).astype(jnp.bfloat16)

def kernel_grad(activation, adjoint, factor):
    active = jax.nn.silu(activation.astype(jnp.float32)).astype(jnp.bfloat16)
    padded = jnp.pad(active, ((0, 0), (1, 1), (1, 1), (0, 0)))
    img_height, img_width, channels = (activation.shape[1], activation.shape[2], activation.shape[3])
    flattened = adjoint.reshape(-1, adjoint.shape[3])
    taps_outer = []
    for tap_row in range(3):
        taps_inner = []
        for tap_col in range(3):
            window = padded[:, tap_row:tap_row + img_height, tap_col:tap_col + img_width, :].reshape(-1, channels)
            taps_inner.append(lax.dot_general(window, flattened, (((0,), (0,)), ((), ())), preferred_element_type=jnp.float32))
        taps_outer.append(jnp.stack(taps_inner))
    return factor * jnp.stack(taps_outer)

def forward_states(start, kernels):
    states = [start]
    for layer in range(STRIDE - 1):
        states.append(advance(states[-1], kernels[layer]))
    return states

def group_first(items):
    start, top_adjoint, kernels = items
    states = forward_states(start, kernels)
    adjoint = top_adjoint
    for layer in range(STRIDE - 1, -1, -1):
        adjoint = retreat(adjoint, states[layer], kernels[layer])
    return adjoint

def shard_grads(activation, adjoint):
    factor = depth_step / BATCH
    act_shards = activation.reshape(N_BATCH, -1, H, W, C)
    adj_shards = adjoint.reshape(N_BATCH, -1, H, W, C)
    total = jnp.zeros((3, 3, C, C), jnp.float32)
    for shard in range(N_BATCH):
        partial_term = kernel_grad(act_shards[shard], adj_shards[shard], factor).astype(jnp.bfloat16)
        partial_term = lax.optimization_barrier(partial_term)
        total = total + partial_term.astype(jnp.float32)
    return total

def group_second(items):
    start, top_adjoint, kernels = items
    states = forward_states(start, kernels)
    adjoint = top_adjoint
    collected = []
    for layer in range(STRIDE - 1, -1, -1):
        collected.append(shard_grads(states[layer], adjoint))
        if layer > 0:
            adjoint = retreat(adjoint, states[layer], kernels[layer])
    return (adjoint, jnp.stack(collected[::-1]))

def reference(u_c, lam_c, weights):
    kernels = weights.reshape(GROUPS, STRIDE, 3, 3, C, C)
    bottoms = lax.map(group_first, (u_c, lam_c, kernels))
    new_top = jnp.concatenate([bottoms[1:], lam_c[-1:]], axis=0)
    lam_low, grads = lax.map(group_second, (u_c, new_top, kernels))
    return (lam_low, grads.reshape(LAYERS, 3, 3, C, C))
```

```python
import functools

import jax
import jax.numpy as jnp
from jax import lax
from jax.experimental import pallas as pl
from jax.experimental.pallas import tpu as pltpu
from jax.sharding import PartitionSpec as P

f32 = jnp.float32
bf16 = jnp.bfloat16
MESH = pl.DeviceIdType.MESH
IMAGES = 8
PAIRS = 16
W = 32
C = 128
K = 3 * C
CHUNK = 288
depth_step = 0.5


def silu_parts(v):
    t = 0.5 * jnp.tanh(0.5 * v) + 0.5
    return v * t, depth_step * (t * (1.0 + v * (1.0 - t)))


def put_rows(x_ref, parity, value):
    column = lax.broadcasted_iota(jnp.int32, value.shape, 1)
    before = jnp.where(column == 0, 0.0, pltpu.roll(value, 1, 1))
    after = jnp.where(column == W - 1, 0.0, pltpu.roll(value, W - 1, 1))
    first = 0 if parity == 0 else 1
    lane = K if parity == 0 else 0
    for b, part in enumerate((before, value, after)):
        x_ref[first : first + PAIRS, :, lane + b * C : lane + (b + 1) * C] = part.astype(bf16)


def clear_edges(x_ref):
    x_ref[0, :, 0:K] = jnp.zeros((W, K), bf16)
    x_ref[PAIRS, :, K : 2 * K] = jnp.zeros((W, K), bf16)


def conv(x_ref, w_ref):
    n = PAIRS * W
    y = jnp.dot(x_ref[0:PAIRS].reshape(n, 2 * K), w_ref[0], preferred_element_type=f32)
    y += jnp.dot(x_ref[1 : PAIRS + 1].reshape(n, 2 * K), w_ref[1], preferred_element_type=f32)
    return y.reshape(PAIRS, W, 2 * C)


def fill_weights(dst, src, layer, transposed):
    for t in range(2):
        for q in range(2):
            for p in range(2):
                a = 2 * t + q - p
                for b in range(3):
                    rows = slice(q * K + b * C, q * K + (b + 1) * C)
                    cols = slice(p * C, (p + 1) * C)
                    if not 0 <= a <= 2:
                        dst[t, rows, cols] = jnp.zeros((C, C), bf16)
                    elif transposed:
                        dst[t, rows, cols] = src[layer, 2 - a, 2 - b].astype(f32).T.astype(bf16)
                    else:
                        dst[t, rows, cols] = src[layer, a, b]


def kernel(
    u_hbm, lam_hbm, w_hbm, low_hbm, grad_hbm,
    u_v, lam_v, w_v, xs0, xs1, xq, xr, g0, g1, bottom, top, a1, low_v, acc,
    wf, wt0, wt1, part, rs_buf, z_own, z_buf, gathered, grad_v,
    u_sem, lam_sem, w_sem, low_sem, grad_sem, send_sem, recv_sem,
    rs_send, rs_recv, z_send, z_recv, ag_send, ag_recv,
):
    layer = lax.axis_index("layer")
    batch = lax.axis_index("batch")
    x, zh = batch // 2, batch % 2
    below, above = jnp.maximum(layer - 1, 0), jnp.minimum(layer + 1, 31)
    has_below, has_above = layer > 0, layer < 31

    def at_x(d):
        return (layer, ((x + d) % 4) * 2 + zh)

    twin = (layer, x * 2 + 1 - zh)

    w_copy = pltpu.make_async_copy(w_hbm, w_v, w_sem)
    w_copy.start()
    for i in range(IMAGES):
        pltpu.make_async_copy(u_hbm.at[i], u_v.at[i], u_sem.at[i]).start()
        pltpu.make_async_copy(lam_hbm.at[i], lam_v.at[i], lam_sem.at[i]).start()

    barrier = pltpu.get_barrier_semaphore()

    @pl.when(has_below)
    def _():
        pl.semaphore_signal(barrier, inc=1, device_id=(below, batch), device_id_type=MESH)

    @pl.when(has_above)
    def _():
        pl.semaphore_signal(barrier, inc=1, device_id=(above, batch), device_id_type=MESH)

    for d in (1, 2, 3):
        pl.semaphore_signal(barrier, inc=1, device_id=at_x(d), device_id_type=MESH)
    pl.semaphore_signal(barrier, inc=1, device_id=twin, device_id_type=MESH)

    clear_edges(xq)
    clear_edges(xr)
    acc[...] = jnp.zeros_like(acc)

    def clear(i, carry):
        clear_edges(xs0.at[i])
        clear_edges(xs1.at[i])
        return carry

    lax.fori_loop(0, IMAGES, clear, 0)
    w_copy.wait()
    fill_weights(wf, w_v, 0, False)
    fill_weights(wt1, w_v, 1, True)
    fill_weights(wt0, w_v, 0, True)

    peers = 4 + jnp.where(has_below, 1, 0) + jnp.where(has_above, 1, 0)
    pl.semaphore_wait(barrier, peers)

    def send_copy(i):
        return pltpu.make_async_remote_copy(
            src_ref=bottom.at[i], dst_ref=top.at[i], send_sem=send_sem.at[i], recv_sem=recv_sem.at[i],
            device_id=(below, batch), device_id_type=MESH,
        )

    def halves(value):
        return value[:, :, :C], value[:, :, C:]

    def first_pass(i, carry):
        pltpu.make_async_copy(u_hbm.at[i], u_v.at[i], u_sem.at[i]).wait()
        for p in range(2):
            s, g = silu_parts(u_v[i, :, p].astype(f32))
            put_rows(xs0.at[i], p, s)
            g0[:, :, p * C : (p + 1) * C] = g
        for p, y in enumerate(halves(conv(xs0.at[i], wf))):
            moved = (u_v[i, :, p].astype(f32) + depth_step * y).astype(bf16).astype(f32)
            s, g = silu_parts(moved)
            put_rows(xs1.at[i], p, s)
            g1[i, :, :, p * C : (p + 1) * C] = g.astype(bf16)
        pltpu.make_async_copy(lam_hbm.at[i], lam_v.at[i], lam_sem.at[i]).wait()
        for p in range(2):
            put_rows(xq, p, lam_v[i, :, p].astype(f32))
        for p, y in enumerate(halves(conv(xq, wt1))):
            g = g1[i, :, :, p * C : (p + 1) * C].astype(f32)
            put_rows(xr, p, (lam_v[i, :, p].astype(f32) + g * y).astype(bf16).astype(f32))
        for p, y in enumerate(halves(conv(xr, wt0))):
            centre = (
                xr[0:PAIRS, :, K + C : K + 2 * C] if p == 0 else xr[1 : PAIRS + 1, :, C : 2 * C]
            )
            bottom[i, :, :, p * C : (p + 1) * C] = (
                centre.astype(f32) + g0[:, :, p * C : (p + 1) * C] * y
            ).astype(bf16)

        @pl.when(has_below)
        def _():
            send_copy(i).start()

        @pl.when(jnp.logical_not(has_above))
        def _():
            for p in range(2):
                top[i, :, :, p * C : (p + 1) * C] = lam_v[i, :, p]

        return carry

    lax.fori_loop(0, IMAGES, first_pass, 0)

    def add_grad(slot, xs, adj, j):
        r = adj[pl.ds(2 * j, 2)].reshape(2 * PAIRS * W, 2 * C)
        for t in range(2):
            patches = xs[pl.ds(2 * j, 2), t : t + PAIRS].reshape(2 * PAIRS * W, 2 * K)
            acc[slot, t] += lax.dot_general(
                patches, r, (((0,), (0,)), ((), ())), preferred_element_type=f32
            )

    def low_copy(i):
        return pltpu.make_async_copy(low_v.at[i], low_hbm.at[i], low_sem.at[i])

    def step_back(i):
        for p in range(2):
            put_rows(xq, p, top[i, :, :, p * C : (p + 1) * C].astype(f32))
        for p, y in enumerate(halves(conv(xq, wt1))):
            cols = slice(p * C, (p + 1) * C)
            moved = top[i, :, :, cols].astype(f32) + g1[i, :, :, cols].astype(f32) * y
            a1[i, :, :, cols] = moved.astype(bf16)
            low_v[i, :, p] = moved.astype(bf16)
        low_copy(i).start()

    def arrived(i):
        @pl.when(has_above)
        def _():
            send_copy(i).wait_recv()

    def second_pass(j, carry):
        arrived(2 * j)
        step_back(2 * j)
        arrived(2 * j + 1)
        add_grad(1, xs1, top, j)

        @pl.when(j == IMAGES // 2 - 1)
        def _():
            scatter(1)

        step_back(2 * j + 1)
        add_grad(0, xs0, a1, j)
        return carry

    factor = depth_step / (IMAGES * 8)

    def rs_copy(slot, d):
        to = (x + d) % 4
        return pltpu.make_async_remote_copy(
            src_ref=part.at[slot, pl.ds(to * CHUNK, CHUNK)], dst_ref=rs_buf.at[slot, d - 1],
            send_sem=rs_send.at[slot, d - 1], recv_sem=rs_recv.at[slot, d - 1],
            device_id=at_x(d), device_id_type=MESH,
        )

    def z_copy(slot):
        return pltpu.make_async_remote_copy(
            src_ref=z_own.at[slot], dst_ref=z_buf.at[slot],
            send_sem=z_send.at[slot], recv_sem=z_recv.at[slot], device_id=twin, device_id_type=MESH,
        )

    def ag_copy(slot, d):
        return pltpu.make_async_remote_copy(
            src_ref=gathered.at[slot, x], dst_ref=gathered.at[slot, x],
            send_sem=ag_send.at[slot, d - 1], recv_sem=ag_recv.at[slot, d - 1],
            device_id=at_x(d), device_id_type=MESH,
        )

    def scatter(slot):
        for a, (one, two) in enumerate((((0, 0, 0), (0, 1, 1)), ((0, 1, 0), (1, 0, 1)), ((1, 0, 0), (1, 1, 1)))):
            total = 0.0
            for t, q, p in (one, two):
                total += acc[slot, t, q * K : (q + 1) * K, p * C : (p + 1) * C]
            part[slot, a * K : (a + 1) * K] = (factor * total).astype(bf16)
        for d in (2, 1, 3):
            rs_copy(slot, d).start()

    def exchange(slot):
        for d in (1, 3, 2):
            rs_copy(slot, d).wait_recv()
        total = part[slot, pl.ds(pl.multiple_of(x * CHUNK, CHUNK), CHUNK)].astype(f32)
        for d in (1, 2, 3):
            total += rs_buf[slot, d - 1].astype(f32)
        z_own[slot] = total.astype(bf16)
        z_copy(slot).start()

    def gather(slot):
        z_copy(slot).wait_recv()
        gathered[slot, x] = (z_own[slot].astype(f32) + z_buf[slot].astype(f32)).astype(bf16)
        for d in (2, 1, 3):
            ag_copy(slot, d).start()

    def grad_copy(slot):
        return pltpu.make_async_copy(grad_v.at[slot], grad_hbm.at[slot], grad_sem.at[slot])

    def finish(slot):
        for d in (1, 3, 2):
            ag_copy(slot, d).wait_recv()
        grad_v[slot] = gathered[slot].astype(f32)
        grad_copy(slot).start()

    lax.fori_loop(0, IMAGES // 2, second_pass, 0)
    scatter(0)
    exchange(1)
    exchange(0)
    gather(1)
    gather(0)
    finish(1)
    finish(0)

    for slot in range(2):
        for d in (1, 2, 3):
            rs_copy(slot, d).wait_send()
            ag_copy(slot, d).wait_send()
        z_copy(slot).wait_send()
        grad_copy(slot).wait()

    def drain(i, carry):
        @pl.when(has_below)
        def _():
            send_copy(i).wait_send()

        low_copy(i).wait()
        return carry

    lax.fori_loop(0, IMAGES, drain, 0)


def body(u_c, lam_c, weights):
    image = (IMAGES, PAIRS, 2, W, C)
    pair = (IMAGES, PAIRS, W, 2 * C)
    patch = (PAIRS + 1, W, 2 * K)
    wide = (2, 2 * K, 2 * C)
    vmem, dma = pltpu.VMEM, pltpu.SemaphoreType.DMA
    low, grad = pl.pallas_call(
        kernel,
        out_shape=(
            jax.ShapeDtypeStruct(image, bf16),
            jax.ShapeDtypeStruct((2, 4, CHUNK, C), f32),
        ),
        in_specs=[pl.BlockSpec(memory_space=pl.ANY)] * 3,
        out_specs=(pl.BlockSpec(memory_space=pl.ANY),) * 2,
        scratch_shapes=[
            vmem(image, bf16), vmem(image, bf16), vmem((2, 3, 3, C, C), bf16),
            vmem((IMAGES,) + patch, bf16), vmem((IMAGES,) + patch, bf16), vmem(patch, bf16), vmem(patch, bf16),
            vmem((PAIRS, W, 2 * C), f32), vmem(pair, bf16),
            vmem(pair, bf16), vmem(pair, bf16), vmem(pair, bf16), vmem(image, bf16),
            vmem((2, 2, 2 * K, 2 * C), f32),
            vmem(wide, bf16), vmem(wide, bf16), vmem(wide, bf16),
            vmem((2, 9 * C, C), bf16), vmem((2, 3, CHUNK, C), bf16),
            vmem((2, CHUNK, C), bf16), vmem((2, CHUNK, C), bf16),
            vmem((2, 4, CHUNK, C), bf16), vmem((2, 4, CHUNK, C), f32),
            dma((IMAGES,)), dma((IMAGES,)), dma, dma((IMAGES,)), dma((2,)),
            dma((IMAGES,)), dma((IMAGES,)),
            dma((2, 3)), dma((2, 3)), dma((2,)), dma((2,)), dma((2, 3)), dma((2, 3)),
        ],
        compiler_params=pltpu.CompilerParams(
            collective_id=0, has_side_effects=True, vmem_limit_bytes=56 * 2**20
        ),
        cost_estimate=pl.CostEstimate(flops=15 * 10**9, bytes_accessed=10**7, transcendentals=2 * 10**6),
        name="relax",
    )(u_c.reshape(image), lam_c.reshape(image), weights)
    return low.reshape(1, IMAGES, 2 * PAIRS, W, C), grad.reshape(2, 3, 3, C, C)


def solution(mesh):
    placed = (
        P("layer", "batch", None, None, None),
        P("layer", "batch", None, None, None),
        P("layer", None, None, None, None),
    )
    return jax.shard_map(
        body,
        mesh=mesh,
        in_specs=placed,
        out_specs=(P("layer", "batch", None, None, None), P("layer", None, None, None, None)),
        check_vma=False,
    )
```

```python
import functools

import jax
import jax.numpy as jnp
from jax import lax
from jax.experimental import pallas as pl
from jax.experimental.pallas import tpu as pltpu
from jax.sharding import PartitionSpec as P

f32 = jnp.float32
bf16 = jnp.bfloat16
MESH = pl.DeviceIdType.MESH
IMAGES = 8
PAIRS = 16
ROWS = 4
CHUNKS = tuple(range(0, PAIRS, ROWS))
W = 32
C = 128
K = 3 * C
CHUNK = 288
PIECES = 2
PIECE = CHUNK // PIECES
TAPS = (((0, 0, 0), (0, 1, 1)), ((0, 1, 0), (1, 0, 1)), ((1, 0, 0), (1, 1, 1)))
depth_step = 0.5


def silu_parts(v):
    t = 0.5 * jnp.tanh(0.5 * v) + 0.5
    return v * t, depth_step * (t * (1.0 + v * (1.0 - t)))


def put_rows(x_ref, at, parity, value):
    column = lax.broadcasted_iota(jnp.int32, value.shape, 1)
    before = jnp.where(column == 0, 0.0, pltpu.roll(value, 1, 1))
    after = jnp.where(column == W - 1, 0.0, pltpu.roll(value, W - 1, 1))
    first = at if parity == 0 else at + 1
    lane = K if parity == 0 else 0
    for b, part in enumerate((before, value, after)):
        x_ref[first : first + ROWS, :, lane + b * C : lane + (b + 1) * C] = part.astype(bf16)


def clear_edges(x_ref):
    x_ref[0, :, 0:K] = jnp.zeros((W, K), bf16)
    x_ref[PAIRS, :, K : 2 * K] = jnp.zeros((W, K), bf16)


def conv(x_ref, w_ref, at):
    n = ROWS * W
    y = jnp.dot(x_ref[at : at + ROWS].reshape(n, 2 * K), w_ref[0], preferred_element_type=f32)
    y += jnp.dot(x_ref[at + 1 : at + ROWS + 1].reshape(n, 2 * K), w_ref[1], preferred_element_type=f32)
    y = y.reshape(ROWS, W, 2 * C)
    return y[:, :, :C], y[:, :, C:]


def fill_weights(dst, src, layer, transposed):
    for t in range(2):
        for q in range(2):
            for p in range(2):
                a = 2 * t + q - p
                for b in range(3):
                    rows = slice(q * K + b * C, q * K + (b + 1) * C)
                    cols = slice(p * C, (p + 1) * C)
                    if not 0 <= a <= 2:
                        dst[t, rows, cols] = jnp.zeros((C, C), bf16)
                    elif transposed:
                        dst[t, rows, cols] = src[layer, 2 - a, 2 - b].astype(f32).T.astype(bf16)
                    else:
                        dst[t, rows, cols] = src[layer, a, b]


def kernel(
    u_hbm, lam_hbm, w_hbm, low_v, summed,
    u_v, lam_v, w_v, xs0, xs1, xq, xr, g0, g1, bottom, top, a1, acc,
    wf, wt0, wt1, part, rs_buf, z_own, z_buf, gathered,
    u_sem, lam_sem, w_sem, send_sem, recv_sem,
    rs_send, rs_recv, z_send, z_recv, ag_send, ag_recv,
):
    layer = lax.axis_index("layer")
    batch = lax.axis_index("batch")
    x, zh = batch // 2, batch % 2
    below, above = jnp.maximum(layer - 1, 0), jnp.minimum(layer + 1, 31)
    has_below, has_above = layer > 0, layer < 31

    def at_x(d):
        return (layer, ((x + d) % 4) * 2 + zh)

    twin = (layer, x * 2 + 1 - zh)

    w_copy = pltpu.make_async_copy(w_hbm, w_v, w_sem)
    w_copy.start()
    for i in range(IMAGES):
        pltpu.make_async_copy(u_hbm.at[i], u_v.at[i], u_sem.at[i]).start()
        pltpu.make_async_copy(lam_hbm.at[i], lam_v.at[i], lam_sem.at[i]).start()

    barrier = pltpu.get_barrier_semaphore()

    @pl.when(has_below)
    def _():
        pl.semaphore_signal(barrier, inc=1, device_id=(below, batch), device_id_type=MESH)

    @pl.when(has_above)
    def _():
        pl.semaphore_signal(barrier, inc=1, device_id=(above, batch), device_id_type=MESH)

    for d in (1, 2, 3):
        pl.semaphore_signal(barrier, inc=1, device_id=at_x(d), device_id_type=MESH)
    pl.semaphore_signal(barrier, inc=1, device_id=twin, device_id_type=MESH)

    clear_edges(xq.at[0])
    clear_edges(xq.at[1])
    clear_edges(xr)
    acc[...] = jnp.zeros_like(acc)

    def clear(i, carry):
        clear_edges(xs0.at[i])
        clear_edges(xs1.at[i])
        return carry

    lax.fori_loop(0, IMAGES, clear, 0)
    w_copy.wait()
    fill_weights(wf, w_v, 0, False)
    fill_weights(wt1, w_v, 1, True)
    fill_weights(wt0, w_v, 0, True)

    peers = 4 + jnp.where(has_below, 1, 0) + jnp.where(has_above, 1, 0)
    pl.semaphore_wait(barrier, peers)

    def send_copy(i):
        return pltpu.make_async_remote_copy(
            src_ref=bottom.at[i], dst_ref=top.at[i], send_sem=send_sem.at[i], recv_sem=recv_sem.at[i],
            device_id=(below, batch), device_id_type=MESH,
        )

    def lanes(p):
        return slice(p * C, (p + 1) * C)

    def load(i):
        pltpu.make_async_copy(u_hbm.at[i], u_v.at[i], u_sem.at[i]).wait()
        pltpu.make_async_copy(lam_hbm.at[i], lam_v.at[i], lam_sem.at[i]).wait()

    def open_state(i, slot, at):
        rows = slice(at, at + ROWS)
        for p in range(2):
            s, g = silu_parts(u_v[i, rows, p].astype(f32))
            put_rows(xs0.at[i], at, p, s)
            g0[slot, rows, :, lanes(p)] = g.astype(bf16)

    def open_adjoint(i, slot, at):
        for p in range(2):
            put_rows(xq.at[slot], at, p, lam_v[i, at : at + ROWS, p].astype(f32))

    def first_pass(i, carry):
        now, then = lax.rem(i, 2), lax.rem(i + 1, 2)
        ahead = jnp.minimum(i + 1, IMAGES - 1)

        @pl.when(i < IMAGES - 1)
        def _():
            load(ahead)

        for at in CHUNKS:
            rows = slice(at, at + ROWS)
            for p, y in enumerate(conv(xs0.at[i], wf, at)):
                moved = (u_v[i, rows, p].astype(f32) + depth_step * y).astype(bf16).astype(f32)
                s, g = silu_parts(moved)
                put_rows(xs1.at[i], at, p, s)
                g1[i, rows, :, lanes(p)] = g.astype(bf16)
        for at in CHUNKS:
            rows = slice(at, at + ROWS)
            for p, y in enumerate(conv(xq.at[now], wt1, at)):
                g = g1[i, rows, :, lanes(p)].astype(f32)
                put_rows(xr, at, p, (lam_v[i, rows, p].astype(f32) + g * y).astype(bf16).astype(f32))
            open_adjoint(ahead, then, at)
        for at in CHUNKS:
            rows = slice(at, at + ROWS)
            for p, y in enumerate(conv(xr, wt0, at)):
                first, lane = (at, K + C) if p == 0 else (at + 1, C)
                centre = xr[first : first + ROWS, :, lane : lane + C].astype(f32)
                g = g0[now, rows, :, lanes(p)].astype(f32)
                bottom[i, rows, :, lanes(p)] = (centre + g * y).astype(bf16)
            open_state(ahead, then, at)

        @pl.when(has_below)
        def _():
            send_copy(i).start()

        @pl.when(jnp.logical_not(has_above))
        def _():
            for p in range(2):
                top[i, :, :, lanes(p)] = lam_v[i, :, p]

        return carry

    load(0)
    for at in CHUNKS:
        open_state(0, 0, at)
        open_adjoint(0, 0, at)
    lax.fori_loop(0, IMAGES, first_pass, 0)

    def add_grad(slot, xs, adj, j):
        r = adj[pl.ds(2 * j, 2)].reshape(2 * PAIRS * W, 2 * C)
        for t in range(2):
            patches = xs[pl.ds(2 * j, 2), t : t + PAIRS].reshape(2 * PAIRS * W, 2 * K)
            acc[slot, t] += lax.dot_general(
                patches, r, (((0,), (0,)), ((), ())), preferred_element_type=f32
            )

    def step_back(i, slot):
        for at in CHUNKS:
            rows = slice(at, at + ROWS)
            for p in range(2):
                put_rows(xq.at[slot], at, p, top[i, rows, :, lanes(p)].astype(f32))
        for at in CHUNKS:
            rows = slice(at, at + ROWS)
            for p, y in enumerate(conv(xq.at[slot], wt1, at)):
                moved = top[i, rows, :, lanes(p)].astype(f32) + g1[i, rows, :, lanes(p)].astype(f32) * y
                a1[i, rows, :, lanes(p)] = moved.astype(bf16)
                low_v[i, rows, p] = moved.astype(bf16)

    def arrived(i):
        @pl.when(has_above)
        def _():
            send_copy(i).wait_recv()

    def second_pass(j, carry):
        arrived(2 * j)
        step_back(2 * j, 0)
        arrived(2 * j + 1)
        add_grad(1, xs1, top, j)

        @pl.when(j == IMAGES // 2 - 1)
        def _():
            scatter(1)

        step_back(2 * j + 1, 1)
        add_grad(0, xs0, a1, j)
        return carry

    factor = depth_step / (IMAGES * 8)

    def piece(k, first=0):
        return pl.ds(pl.multiple_of(first + k * PIECE, 16), PIECE)

    def rs_copy(slot, k, d):
        to = (x + d) % 4
        return pltpu.make_async_remote_copy(
            src_ref=part.at[slot, piece(k, to * CHUNK)], dst_ref=rs_buf.at[slot, d - 1, piece(k)],
            send_sem=rs_send.at[slot, k, d - 1], recv_sem=rs_recv.at[slot, k, d - 1],
            device_id=at_x(d), device_id_type=MESH,
        )

    def z_copy(slot, k):
        return pltpu.make_async_remote_copy(
            src_ref=z_own.at[slot, piece(k)], dst_ref=z_buf.at[slot, piece(k)],
            send_sem=z_send.at[slot, k], recv_sem=z_recv.at[slot, k],
            device_id=twin, device_id_type=MESH,
        )

    def ag_copy(slot, k, d):
        return pltpu.make_async_remote_copy(
            src_ref=gathered.at[slot, x, piece(k)], dst_ref=gathered.at[slot, x, piece(k)],
            send_sem=ag_send.at[slot, k, d - 1], recv_sem=ag_recv.at[slot, k, d - 1],
            device_id=at_x(d), device_id_type=MESH,
        )

    def scatter(slot):
        for a, terms in enumerate(TAPS):
            total = 0.0
            for t, q, p in terms:
                total += acc[slot, t, q * K : (q + 1) * K, lanes(p)]
            part[slot, a * K : (a + 1) * K] = (factor * total).astype(bf16)
        for k in range(PIECES):
            for d in (2, 1, 3):
                rs_copy(slot, k, d).start()

    def exchange(slot, k):
        for d in (1, 3, 2):
            rs_copy(slot, k, d).wait_recv()
        total = part[slot, piece(k, x * CHUNK)].astype(f32)
        for d in (1, 2, 3):
            total += rs_buf[slot, d - 1, piece(k)].astype(f32)
        z_own[slot, piece(k)] = total.astype(bf16)
        z_copy(slot, k).start()

    def gather(slot, k):
        z_copy(slot, k).wait_recv()
        total = z_own[slot, piece(k)].astype(f32) + z_buf[slot, piece(k)].astype(f32)
        gathered[slot, x, piece(k)] = total.astype(bf16)
        for d in (2, 1, 3):
            ag_copy(slot, k, d).start()

    def finish(slot):
        for k in range(PIECES):
            for d in (1, 3, 2):
                ag_copy(slot, k, d).wait_recv()
        summed[slot] = gathered[slot]

    lax.fori_loop(0, IMAGES // 2, second_pass, 0)
    scatter(0)
    order = [(slot, k) for slot in (1, 0) for k in range(PIECES)]
    for n in range(len(order) + PIECES):
        if n < len(order):
            exchange(*order[n])
        if n >= PIECES:
            gather(*order[n - PIECES])
    finish(1)
    finish(0)

    for slot in range(2):
        for k in range(PIECES):
            for d in (1, 2, 3):
                rs_copy(slot, k, d).wait_send()
                ag_copy(slot, k, d).wait_send()
            z_copy(slot, k).wait_send()

    def drain(i, carry):
        @pl.when(has_below)
        def _():
            send_copy(i).wait_send()

        return carry

    lax.fori_loop(0, IMAGES, drain, 0)


def deliver(low_v, sum_v, low_out, grad_out, grad_v, low_sem, grad_sem):
    def low_copy(i):
        return pltpu.make_async_copy(low_v.at[i], low_out.at[i], low_sem.at[i])

    def grad_copy(slot):
        return pltpu.make_async_copy(grad_v.at[slot], grad_out.at[slot], grad_sem.at[slot])

    for i in range(IMAGES):
        low_copy(i).start()
    for slot in range(2):
        grad_v[slot] = sum_v[slot].astype(f32)
        grad_copy(slot).start()
    for slot in range(2):
        grad_copy(slot).wait()
    for i in range(IMAGES):
        low_copy(i).wait()


def body(u_c, lam_c, weights):
    image = (IMAGES, PAIRS, 2, W, C)
    pair = (IMAGES, PAIRS, W, 2 * C)
    patch = (PAIRS + 1, W, 2 * K)
    wide = (2, 2 * K, 2 * C)
    vmem, dma = pltpu.VMEM, pltpu.SemaphoreType.DMA
    low, grad = pl.pallas_call(
        kernel,
        out_shape=(pltpu.VMEM(image, bf16), pltpu.VMEM((2, 4, CHUNK, C), bf16)),
        in_specs=[pl.BlockSpec(memory_space=pl.ANY)] * 3,
        out_specs=(pl.BlockSpec(memory_space=vmem),) * 2,
        scratch_shapes=[
            vmem(image, bf16), vmem(image, bf16), vmem((2, 3, 3, C, C), bf16),
            vmem((IMAGES,) + patch, bf16), vmem((IMAGES,) + patch, bf16), vmem((2,) + patch, bf16), vmem(patch, bf16),
            vmem((2, PAIRS, W, 2 * C), bf16), vmem(pair, bf16),
            vmem(pair, bf16), vmem(pair, bf16), vmem(pair, bf16),
            vmem((2, 2, 2 * K, 2 * C), f32),
            vmem(wide, bf16), vmem(wide, bf16), vmem(wide, bf16),
            vmem((2, 9 * C, C), bf16), vmem((2, 3, CHUNK, C), bf16),
            vmem((2, CHUNK, C), bf16), vmem((2, CHUNK, C), bf16),
            vmem((2, 4, CHUNK, C), bf16),
            dma((IMAGES,)), dma((IMAGES,)), dma,
            dma((IMAGES,)), dma((IMAGES,)),
            dma((2, PIECES, 3)), dma((2, PIECES, 3)), dma((2, PIECES)), dma((2, PIECES)),
            dma((2, PIECES, 3)), dma((2, PIECES, 3)),
        ],
        compiler_params=pltpu.CompilerParams(
            collective_id=0, has_side_effects=True, vmem_limit_bytes=52 * 2**20
        ),
        cost_estimate=pl.CostEstimate(flops=15 * 10**9, bytes_accessed=10**7, transcendentals=2 * 10**6),
        name="relax",
    )(u_c.reshape(image), lam_c.reshape(image), weights)
    low, grad = pl.pallas_call(
        deliver,
        out_shape=(
            jax.ShapeDtypeStruct(image, bf16),
            jax.ShapeDtypeStruct((2, 4, CHUNK, C), f32),
        ),
        in_specs=[pl.BlockSpec(memory_space=vmem)] * 2,
        out_specs=(pl.BlockSpec(memory_space=pl.ANY),) * 2,
        scratch_shapes=[vmem((2, 4, CHUNK, C), f32), dma((IMAGES,)), dma((2,))],
        compiler_params=pltpu.CompilerParams(vmem_limit_bytes=8 * 2**20),
        name="deliver",
    )(low, grad)
    return low.reshape(1, IMAGES, 2 * PAIRS, W, C), grad.reshape(2, 3, 3, C, C)


def solution(mesh):
    placed = (
        P("layer", "batch", None, None, None),
        P("layer", "batch", None, None, None),
        P("layer", None, None, None, None),
    )
    return jax.shard_map(
        body,
        mesh=mesh,
        in_specs=placed,
        out_specs=(P("layer", "batch", None, None, None), P("layer", None, None, None, None)),
        check_vma=False,
    )
```

```python
import functools

import jax
import jax.numpy as jnp
from jax import lax
from jax.experimental import pallas as pl
from jax.experimental.pallas import tpu as pltpu
from jax.sharding import PartitionSpec as P

f32 = jnp.float32
bf16 = jnp.bfloat16
MESH = pl.DeviceIdType.MESH
IMAGES = 8
PAIRS = 16
ROWS = 4
CHUNKS = tuple(range(0, PAIRS, ROWS))
W = 32
C = 128
K = 3 * C
CHUNK = 288
PIECES = 2
PIECE = CHUNK // PIECES
TAPS = (((0, 0, 0), (0, 1, 1)), ((0, 1, 0), (1, 0, 1)), ((1, 0, 0), (1, 1, 1)))
depth_step = 0.5


def silu_parts(v):
    t = 0.5 * jnp.tanh(0.5 * v) + 0.5
    return v * t, depth_step * (t * (1.0 + v * (1.0 - t)))


def put_rows(x_ref, at, parity, value):
    column = lax.broadcasted_iota(jnp.int32, value.shape, 1)
    before = jnp.where(column == 0, 0.0, pltpu.roll(value, 1, 1))
    after = jnp.where(column == W - 1, 0.0, pltpu.roll(value, W - 1, 1))
    first = at if parity == 0 else at + 1
    lane = K if parity == 0 else 0
    for b, part in enumerate((before, value, after)):
        x_ref[first : first + ROWS, :, lane + b * C : lane + (b + 1) * C] = part.astype(bf16)


def clear_edges(x_ref):
    x_ref[0, :, 0:K] = jnp.zeros((W, K), bf16)
    x_ref[PAIRS, :, K : 2 * K] = jnp.zeros((W, K), bf16)


def conv(x_ref, w_ref, at):
    n = ROWS * W
    y = jnp.dot(x_ref[at : at + ROWS].reshape(n, 2 * K), w_ref[0], preferred_element_type=f32)
    y += jnp.dot(x_ref[at + 1 : at + ROWS + 1].reshape(n, 2 * K), w_ref[1], preferred_element_type=f32)
    y = y.reshape(ROWS, W, 2 * C)
    return y[:, :, :C], y[:, :, C:]


def fill_weights(dst, src, layer, transposed):
    for t in range(2):
        for q in range(2):
            for p in range(2):
                a = 2 * t + q - p
                for b in range(3):
                    rows = slice(q * K + b * C, q * K + (b + 1) * C)
                    cols = slice(p * C, (p + 1) * C)
                    if not 0 <= a <= 2:
                        dst[t, rows, cols] = jnp.zeros((C, C), bf16)
                    elif transposed:
                        dst[t, rows, cols] = src[layer, 2 - a, 2 - b].T
                    else:
                        dst[t, rows, cols] = src[layer, a, b]


def kernel(
    u_hbm, lam_hbm, w_hbm, low_v, summed,
    u_v, lam_v, w_v, xs0, xs1, xq, xr, g0, g1, bottom, top, a1, acc,
    wf, wt0, wt1, part, rs_buf, z_own, z_buf, gathered,
    u_sem, lam_sem, w_sem, send_sem, recv_sem,
    rs_send, rs_recv, z_send, z_recv, ag_send, ag_recv,
):
    layer = lax.axis_index("layer")
    batch = lax.axis_index("batch")
    x, zh = batch // 2, batch % 2
    below, above = jnp.maximum(layer - 1, 0), jnp.minimum(layer + 1, 31)
    has_below, has_above = layer > 0, layer < 31

    def at_x(d):
        return (layer, ((x + d) % 4) * 2 + zh)

    twin = (layer, x * 2 + 1 - zh)

    def w_copy(slot):
        return pltpu.make_async_copy(w_hbm.at[slot], w_v.at[slot], w_sem.at[slot])

    def u_copy(i):
        return pltpu.make_async_copy(u_hbm.at[i], u_v.at[i], u_sem.at[i])

    def lam_copy(i):
        return pltpu.make_async_copy(lam_hbm.at[i], lam_v.at[i], lam_sem.at[i])

    u_copy(0).start()
    w_copy(0).start()
    lam_copy(0).start()
    w_copy(1).start()
    barrier = pltpu.get_barrier_semaphore()

    @pl.when(has_below)
    def _():
        pl.semaphore_signal(barrier, inc=1, device_id=(below, batch), device_id_type=MESH)

    @pl.when(has_above)
    def _():
        pl.semaphore_signal(barrier, inc=1, device_id=(above, batch), device_id_type=MESH)

    for d in (1, 2, 3):
        pl.semaphore_signal(barrier, inc=1, device_id=at_x(d), device_id_type=MESH)
    pl.semaphore_signal(barrier, inc=1, device_id=twin, device_id_type=MESH)

    clear_edges(xq.at[0])
    clear_edges(xq.at[1])
    clear_edges(xr)
    acc[...] = jnp.zeros_like(acc)

    def clear(i, carry):
        clear_edges(xs0.at[i])
        clear_edges(xs1.at[i])
        return carry

    lax.fori_loop(0, IMAGES, clear, 0)
    def send_copy(i):
        return pltpu.make_async_remote_copy(
            src_ref=bottom.at[i], dst_ref=top.at[i], send_sem=send_sem.at[i], recv_sem=recv_sem.at[i],
            device_id=(below, batch), device_id_type=MESH,
        )

    def lanes(p):
        return slice(p * C, (p + 1) * C)

    def load(i):
        u_copy(i).wait()
        lam_copy(i).wait()

    def open_state(i, slot, at):
        rows = slice(at, at + ROWS)
        for p in range(2):
            s, g = silu_parts(u_v[i, rows, p].astype(f32))
            put_rows(xs0.at[i], at, p, s)
            g0[slot, rows, :, lanes(p)] = g.astype(bf16)

    def open_adjoint(i, slot, at):
        for p in range(2):
            put_rows(xq.at[slot], at, p, lam_v[i, at : at + ROWS, p].astype(f32))

    def first_pass(i, carry):
        now, then = lax.rem(i, 2), lax.rem(i + 1, 2)
        ahead = jnp.minimum(i + 1, IMAGES - 1)

        @pl.when(i < IMAGES - 1)
        def _():
            load(ahead)

        for at in CHUNKS:
            rows = slice(at, at + ROWS)
            for p, y in enumerate(conv(xs0.at[i], wf, at)):
                moved = (u_v[i, rows, p].astype(f32) + depth_step * y).astype(bf16).astype(f32)
                s, g = silu_parts(moved)
                put_rows(xs1.at[i], at, p, s)
                g1[i, rows, :, lanes(p)] = g.astype(bf16)
        for at in CHUNKS:
            rows = slice(at, at + ROWS)
            for p, y in enumerate(conv(xq.at[now], wt1, at)):
                g = g1[i, rows, :, lanes(p)].astype(f32)
                put_rows(xr, at, p, (lam_v[i, rows, p].astype(f32) + g * y).astype(bf16).astype(f32))
            open_adjoint(ahead, then, at)
        for at in CHUNKS:
            rows = slice(at, at + ROWS)
            for p, y in enumerate(conv(xr, wt0, at)):
                first, lane = (at, K + C) if p == 0 else (at + 1, C)
                centre = xr[first : first + ROWS, :, lane : lane + C].astype(f32)
                g = g0[now, rows, :, lanes(p)].astype(f32)
                bottom[i, rows, :, lanes(p)] = (centre + g * y).astype(bf16)
            open_state(ahead, then, at)

        @pl.when(has_below)
        def _():
            send_copy(i).start()

        @pl.when(jnp.logical_not(has_above))
        def _():
            for p in range(2):
                top[i, :, :, lanes(p)] = lam_v[i, :, p]

        return carry

    load(0)
    w_copy(0).wait()
    w_copy(1).wait()
    for i in range(1, IMAGES):
        u_copy(i).start()
        lam_copy(i).start()
    fill_weights(wf, w_v, 0, False)
    for at in CHUNKS:
        open_state(0, 0, at)
        open_adjoint(0, 0, at)
    fill_weights(wt1, w_v, 1, True)
    fill_weights(wt0, w_v, 0, True)
    peers = 4 + jnp.where(has_below, 1, 0) + jnp.where(has_above, 1, 0)
    pl.semaphore_wait(barrier, peers)

    lax.fori_loop(0, IMAGES, first_pass, 0)

    def add_grad(slot, xs, adj, i, count):
        n = count * PAIRS * W
        r = adj[pl.ds(i, count)].reshape(n, 2 * C)
        for t in range(2):
            patches = xs[pl.ds(i, count), t : t + PAIRS].reshape(n, 2 * K)
            acc[slot, t] += lax.dot_general(
                patches, r, (((0,), (0,)), ((), ())), preferred_element_type=f32
            )

    def step_back(i, slot):
        for at in CHUNKS:
            rows = slice(at, at + ROWS)
            for p in range(2):
                put_rows(xq.at[slot], at, p, top[i, rows, :, lanes(p)].astype(f32))
        for at in CHUNKS:
            rows = slice(at, at + ROWS)
            for p, y in enumerate(conv(xq.at[slot], wt1, at)):
                moved = top[i, rows, :, lanes(p)].astype(f32) + g1[i, rows, :, lanes(p)].astype(f32) * y
                a1[i, rows, :, lanes(p)] = moved.astype(bf16)
                low_v[i, rows, p] = moved.astype(bf16)

    def arrived(i):
        @pl.when(has_above)
        def _():
            send_copy(i).wait_recv()

    def second_pass(j, carry):
        for slot in range(2):
            arrived(2 * j + slot)
            step_back(2 * j + slot, slot)
        add_grad(1, xs1, top, 2 * j, 2)
        add_grad(0, xs0, a1, 2 * j, 2)
        return carry

    factor = depth_step / (IMAGES * 8)

    def piece(k, first=0):
        return pl.ds(pl.multiple_of(first + k * PIECE, 16), PIECE)

    def rs_copy(slot, k, d):
        to = (x + d) % 4
        return pltpu.make_async_remote_copy(
            src_ref=part.at[slot, piece(k, to * CHUNK)], dst_ref=rs_buf.at[slot, d - 1, piece(k)],
            send_sem=rs_send.at[slot, k, d - 1], recv_sem=rs_recv.at[slot, k, d - 1],
            device_id=at_x(d), device_id_type=MESH,
        )

    def z_copy(slot, k):
        return pltpu.make_async_remote_copy(
            src_ref=z_own.at[slot, piece(k)], dst_ref=z_buf.at[slot, piece(k)],
            send_sem=z_send.at[slot, k], recv_sem=z_recv.at[slot, k],
            device_id=twin, device_id_type=MESH,
        )

    def ag_copy(slot, k, d):
        return pltpu.make_async_remote_copy(
            src_ref=gathered.at[slot, x, piece(k)], dst_ref=gathered.at[slot, x, piece(k)],
            send_sem=ag_send.at[slot, k, d - 1], recv_sem=ag_recv.at[slot, k, d - 1],
            device_id=at_x(d), device_id_type=MESH,
        )

    def scatter(slot):
        for a, terms in enumerate(TAPS):
            total = 0.0
            for t, q, p in terms:
                total += acc[slot, t, q * K : (q + 1) * K, lanes(p)]
            part[slot, a * K : (a + 1) * K] = (factor * total).astype(bf16)
        for k in range(PIECES):
            for d in (2, 1, 3):
                rs_copy(slot, k, d).start()

    def exchange(slot, k):
        for d in (1, 3, 2):
            rs_copy(slot, k, d).wait_recv()
        total = part[slot, piece(k, x * CHUNK)].astype(f32)
        for d in (1, 2, 3):
            total += rs_buf[slot, d - 1, piece(k)].astype(f32)
        z_own[slot, piece(k)] = total.astype(bf16)
        z_copy(slot, k).start()

    def gather(slot, k):
        z_copy(slot, k).wait_recv()
        total = z_own[slot, piece(k)].astype(f32) + z_buf[slot, piece(k)].astype(f32)
        gathered[slot, x, piece(k)] = total.astype(bf16)
        for d in (2, 1, 3):
            ag_copy(slot, k, d).start()

    def finish(slot):
        for k in range(PIECES):
            for d in (1, 3, 2):
                ag_copy(slot, k, d).wait_recv()
        summed[slot] = gathered[slot]

    lax.fori_loop(0, IMAGES // 2 - 1, second_pass, 0)
    for i in (IMAGES - 2, IMAGES - 1):
        arrived(i)
        add_grad(1, xs1, top, i, 1)
        if i == IMAGES - 1:
            scatter(1)
        step_back(i, i % 2)
        add_grad(0, xs0, a1, i, 1)
    scatter(0)
    order = [(slot, k) for slot in (1, 0) for k in range(PIECES)]
    for n in range(len(order) + PIECES):
        if n < len(order):
            exchange(*order[n])
        if n >= PIECES:
            gather(*order[n - PIECES])
    finish(1)
    finish(0)

    for slot in range(2):
        for k in range(PIECES):
            for d in (1, 2, 3):
                rs_copy(slot, k, d).wait_send()
                ag_copy(slot, k, d).wait_send()
            z_copy(slot, k).wait_send()

    def drain(i, carry):
        @pl.when(has_below)
        def _():
            send_copy(i).wait_send()

        return carry

    lax.fori_loop(0, IMAGES, drain, 0)


def deliver(low_v, sum_v, low_out, grad_out, grad_v, low_sem, grad_sem):
    def low_copy(i):
        return pltpu.make_async_copy(low_v.at[i], low_out.at[i], low_sem.at[i])

    def grad_copy(slot):
        return pltpu.make_async_copy(grad_v.at[slot], grad_out.at[slot], grad_sem.at[slot])

    for i in range(IMAGES):
        low_copy(i).start()
    for slot in range(2):
        grad_v[slot] = sum_v[slot].astype(f32)
        grad_copy(slot).start()
    for slot in range(2):
        grad_copy(slot).wait()
    for i in range(IMAGES):
        low_copy(i).wait()


def body(u_c, lam_c, weights):
    image = (IMAGES, PAIRS, 2, W, C)
    pair = (IMAGES, PAIRS, W, 2 * C)
    patch = (PAIRS + 1, W, 2 * K)
    wide = (2, 2 * K, 2 * C)
    vmem, dma = pltpu.VMEM, pltpu.SemaphoreType.DMA
    low, grad = pl.pallas_call(
        kernel,
        out_shape=(pltpu.VMEM(image, bf16), pltpu.VMEM((2, 4, CHUNK, C), bf16)),
        in_specs=[pl.BlockSpec(memory_space=pl.ANY)] * 3,
        out_specs=(pl.BlockSpec(memory_space=vmem),) * 2,
        scratch_shapes=[
            vmem(image, bf16), vmem(image, bf16), vmem((2, 3, 3, C, C), bf16),
            vmem((IMAGES,) + patch, bf16), vmem((IMAGES,) + patch, bf16), vmem((2,) + patch, bf16), vmem(patch, bf16),
            vmem((2, PAIRS, W, 2 * C), bf16), vmem(pair, bf16),
            vmem(pair, bf16), vmem(pair, bf16), vmem(pair, bf16),
            vmem((2, 2, 2 * K, 2 * C), f32),
            vmem(wide, bf16), vmem(wide, bf16), vmem(wide, bf16),
            vmem((2, 9 * C, C), bf16), vmem((2, 3, CHUNK, C), bf16),
            vmem((2, CHUNK, C), bf16), vmem((2, CHUNK, C), bf16),
            vmem((2, 4, CHUNK, C), bf16),
            dma((IMAGES,)), dma((IMAGES,)), dma((2,)),
            dma((IMAGES,)), dma((IMAGES,)),
            dma((2, PIECES, 3)), dma((2, PIECES, 3)), dma((2, PIECES)), dma((2, PIECES)),
            dma((2, PIECES, 3)), dma((2, PIECES, 3)),
        ],
        compiler_params=pltpu.CompilerParams(
            collective_id=0, has_side_effects=True, vmem_limit_bytes=52 * 2**20
        ),
        cost_estimate=pl.CostEstimate(flops=15 * 10**9, bytes_accessed=10**7, transcendentals=2 * 10**6),
        name="relax",
    )(u_c.reshape(image), lam_c.reshape(image), weights)
    low, grad = pl.pallas_call(
        deliver,
        out_shape=(
            jax.ShapeDtypeStruct(image, bf16),
            jax.ShapeDtypeStruct((2, 4, CHUNK, C), f32),
        ),
        in_specs=[pl.BlockSpec(memory_space=vmem)] * 2,
        out_specs=(pl.BlockSpec(memory_space=pl.ANY),) * 2,
        scratch_shapes=[vmem((2, 4, CHUNK, C), f32), dma((IMAGES,)), dma((2,))],
        compiler_params=pltpu.CompilerParams(vmem_limit_bytes=8 * 2**20),
        name="deliver",
    )(low, grad)
    return low.reshape(1, IMAGES, 2 * PAIRS, W, C), grad.reshape(2, 3, 3, C, C)


def solution(mesh):
    placed = (
        P("layer", "batch", None, None, None),
        P("layer", "batch", None, None, None),
        P("layer", None, None, None, None),
    )
    return jax.shard_map(
        body,
        mesh=mesh,
        in_specs=placed,
        out_specs=(P("layer", "batch", None, None, None), P("layer", None, None, None, None)),
        check_vma=False,
    )
```

```python
import functools

import jax
import jax.numpy as jnp
from jax import lax
from jax.experimental import pallas as pl
from jax.experimental.pallas import tpu as pltpu
from jax.sharding import PartitionSpec as P

f32 = jnp.float32
bf16 = jnp.bfloat16
MESH = pl.DeviceIdType.MESH
IMAGES = 8
PAIRS = 16
ROWS = 8
CHUNKS = tuple(range(0, PAIRS, ROWS))
W = 32
C = 128
K = 3 * C
CHUNK = 288
PIECES = 2
PIECE = CHUNK // PIECES
TAPS = (((0, 0, 0), (0, 1, 1)), ((0, 1, 0), (1, 0, 1)), ((1, 0, 0), (1, 1, 1)))
depth_step = 0.5


def silu_parts(v):
    t = 0.5 * jnp.tanh(0.5 * v) + 0.5
    return v * t, depth_step * (t * (1.0 + v * (1.0 - t)))


def put_rows(x_ref, at, parity, value):
    column = lax.broadcasted_iota(jnp.int32, value.shape, 1)
    before = jnp.where(column == 0, 0.0, pltpu.roll(value, 1, 1))
    after = jnp.where(column == W - 1, 0.0, pltpu.roll(value, W - 1, 1))
    first = at if parity == 0 else at + 1
    lane = K if parity == 0 else 0
    for b, part in enumerate((before, value, after)):
        x_ref[first : first + ROWS, :, lane + b * C : lane + (b + 1) * C] = part.astype(bf16)


def clear_edges(x_ref):
    x_ref[0, :, 0:K] = jnp.zeros((W, K), bf16)
    x_ref[PAIRS, :, K : 2 * K] = jnp.zeros((W, K), bf16)


def conv(x_ref, w_ref, at):
    n = ROWS // 2 * W
    d = x_ref[at : at + ROWS].reshape(ROWS // 2, 2, W, 2 * K)
    later = x_ref[at + 1 : at + ROWS + 1].reshape(ROWS // 2, 2, W, 2 * K)
    d0, d1, d2 = (v.reshape(n, 2 * K) for v in (d[:, 0], d[:, 1], later[:, 1]))
    shared = jnp.dot(d1, w_ref[1], preferred_element_type=f32)
    upper = shared + jnp.dot(d0 - d1, w_ref[0], preferred_element_type=f32)
    lower = shared + jnp.dot(d2 - d1, w_ref[2], preferred_element_type=f32)
    shape = (ROWS // 2, W, 2 * C)
    y = jnp.stack([upper.reshape(shape), lower.reshape(shape)], axis=1).reshape(ROWS, W, 2 * C)
    return y[:, :, :C], y[:, :, C:]


def fill_weights(dst, src, layer, transposed):
    for t in range(2):
        for q in range(2):
            for p in range(2):
                a = 2 * t + q - p
                for b in range(3):
                    rows = slice(q * K + b * C, q * K + (b + 1) * C)
                    cols = slice(p * C, (p + 1) * C)
                    if not 0 <= a <= 2:
                        dst[2 * t, rows, cols] = jnp.zeros((C, C), bf16)
                    elif transposed:
                        dst[2 * t, rows, cols] = src[layer, 2 - a, 2 - b].T
                    else:
                        dst[2 * t, rows, cols] = src[layer, a, b]
    dst[1] = dst[0] + dst[2]


def kernel(
    u_hbm, lam_hbm, w_hbm, low_v, summed,
    u_v, lam_v, w_v, xs0, xs1, xq, xr, g0, g1, bottom, top, a1, acc,
    wf, wt0, wt1, part, rs_buf, z_own, z_buf, gathered,
    u_sem, lam_sem, w_sem, send_sem, recv_sem,
    rs_send, rs_recv, z_send, z_recv, ag_send, ag_recv,
):
    layer = lax.axis_index("layer")
    batch = lax.axis_index("batch")
    x, zh = batch // 2, batch % 2
    below, above = jnp.maximum(layer - 1, 0), jnp.minimum(layer + 1, 31)
    has_below, has_above = layer > 0, layer < 31

    def at_x(d):
        return (layer, ((x + d) % 4) * 2 + zh)

    twin = (layer, x * 2 + 1 - zh)

    def w_copy(slot):
        return pltpu.make_async_copy(w_hbm.at[slot], w_v.at[slot], w_sem.at[slot])

    def u_copy(i):
        return pltpu.make_async_copy(u_hbm.at[i], u_v.at[i], u_sem.at[i])

    def lam_copy(i):
        return pltpu.make_async_copy(lam_hbm.at[i], lam_v.at[i], lam_sem.at[i])

    u_copy(0).start()
    w_copy(0).start()
    lam_copy(0).start()
    w_copy(1).start()
    barrier = pltpu.get_barrier_semaphore()

    @pl.when(has_below)
    def _():
        pl.semaphore_signal(barrier, inc=1, device_id=(below, batch), device_id_type=MESH)

    @pl.when(has_above)
    def _():
        pl.semaphore_signal(barrier, inc=1, device_id=(above, batch), device_id_type=MESH)

    for d in (1, 2, 3):
        pl.semaphore_signal(barrier, inc=1, device_id=at_x(d), device_id_type=MESH)
    pl.semaphore_signal(barrier, inc=1, device_id=twin, device_id_type=MESH)

    clear_edges(xq.at[0])
    clear_edges(xq.at[1])
    clear_edges(xr)
    acc[...] = jnp.zeros_like(acc)

    def clear(i, carry):
        clear_edges(xs0.at[i])
        clear_edges(xs1.at[i])
        return carry

    lax.fori_loop(0, IMAGES, clear, 0)
    def send_copy(i):
        return pltpu.make_async_remote_copy(
            src_ref=bottom.at[i], dst_ref=top.at[i], send_sem=send_sem.at[i], recv_sem=recv_sem.at[i],
            device_id=(below, batch), device_id_type=MESH,
        )

    def lanes(p):
        return slice(p * C, (p + 1) * C)

    def load(i):
        u_copy(i).wait()
        lam_copy(i).wait()

    def open_state(i, slot, at):
        rows = slice(at, at + ROWS)
        for p in range(2):
            s, g = silu_parts(u_v[i, rows, p].astype(f32))
            put_rows(xs0.at[i], at, p, s)
            g0[slot, rows, :, lanes(p)] = g.astype(bf16)

    def open_adjoint(i, slot, at):
        for p in range(2):
            put_rows(xq.at[slot], at, p, lam_v[i, at : at + ROWS, p].astype(f32))

    def first_pass(i, carry):
        now, then = lax.rem(i, 2), lax.rem(i + 1, 2)
        ahead = jnp.minimum(i + 1, IMAGES - 1)

        @pl.when(i < IMAGES - 1)
        def _():
            load(ahead)

        for at in CHUNKS:
            rows = slice(at, at + ROWS)
            for p, y in enumerate(conv(xs0.at[i], wf, at)):
                moved = (u_v[i, rows, p].astype(f32) + depth_step * y).astype(bf16).astype(f32)
                s, g = silu_parts(moved)
                put_rows(xs1.at[i], at, p, s)
                g1[i, rows, :, lanes(p)] = g.astype(bf16)
        for at in CHUNKS:
            rows = slice(at, at + ROWS)
            for p, y in enumerate(conv(xq.at[now], wt1, at)):
                g = g1[i, rows, :, lanes(p)].astype(f32)
                put_rows(xr, at, p, (lam_v[i, rows, p].astype(f32) + g * y).astype(bf16).astype(f32))
            open_adjoint(ahead, then, at)
        for at in CHUNKS:
            rows = slice(at, at + ROWS)
            for p, y in enumerate(conv(xr, wt0, at)):
                first, lane = (at, K + C) if p == 0 else (at + 1, C)
                centre = xr[first : first + ROWS, :, lane : lane + C].astype(f32)
                g = g0[now, rows, :, lanes(p)].astype(f32)
                bottom[i, rows, :, lanes(p)] = (centre + g * y).astype(bf16)
            open_state(ahead, then, at)

        @pl.when(has_below)
        def _():
            send_copy(i).start()

        @pl.when(jnp.logical_not(has_above))
        def _():
            for p in range(2):
                top[i, :, :, lanes(p)] = lam_v[i, :, p]

        return carry

    load(0)
    w_copy(0).wait()
    w_copy(1).wait()
    for i in range(1, IMAGES):
        u_copy(i).start()
        lam_copy(i).start()
    fill_weights(wf, w_v, 0, False)
    for at in CHUNKS:
        open_state(0, 0, at)
        open_adjoint(0, 0, at)
    fill_weights(wt1, w_v, 1, True)
    fill_weights(wt0, w_v, 0, True)
    peers = 4 + jnp.where(has_below, 1, 0) + jnp.where(has_above, 1, 0)
    pl.semaphore_wait(barrier, peers)

    lax.fori_loop(0, IMAGES, first_pass, 0)

    def add_grad(slot, xs, adj, i, count):
        n = count * PAIRS // 2 * W
        r = adj[pl.ds(i, count)].reshape(count, PAIRS // 2, 2, W, 2 * C)
        d = xs[pl.ds(i, count), 0:PAIRS].reshape(count, PAIRS // 2, 2, W, 2 * K)
        later = xs[pl.ds(i, count), 1 : PAIRS + 1].reshape(count, PAIRS // 2, 2, W, 2 * K)
        r0, r1 = r[:, :, 0], r[:, :, 1]
        d0, d1, d2 = d[:, :, 0], d[:, :, 1], later[:, :, 1]
        for t, (left, right) in enumerate(((d0 - d1, r0), (d1, r0 + r1), (d2 - d1, r1))):
            acc[slot, t] += lax.dot_general(
                left.reshape(n, 2 * K), right.reshape(n, 2 * C),
                (((0,), (0,)), ((), ())), preferred_element_type=f32,
            )

    def step_back(i, slot):
        for at in CHUNKS:
            rows = slice(at, at + ROWS)
            for p in range(2):
                put_rows(xq.at[slot], at, p, top[i, rows, :, lanes(p)].astype(f32))
        for at in CHUNKS:
            rows = slice(at, at + ROWS)
            for p, y in enumerate(conv(xq.at[slot], wt1, at)):
                moved = top[i, rows, :, lanes(p)].astype(f32) + g1[i, rows, :, lanes(p)].astype(f32) * y
                a1[i, rows, :, lanes(p)] = moved.astype(bf16)
                low_v[i, rows, p] = moved.astype(bf16)

    def arrived(i):
        @pl.when(has_above)
        def _():
            send_copy(i).wait_recv()

    def second_pass(j, carry):
        for slot in range(2):
            arrived(2 * j + slot)
            step_back(2 * j + slot, slot)
        add_grad(1, xs1, top, 2 * j, 2)

        @pl.when(j < 2)
        def _():
            add_grad(0, xs0, a1, 2 * j, 2)

        return carry

    factor = depth_step / (IMAGES * 8)

    def piece(k, first=0):
        return pl.ds(pl.multiple_of(first + k * PIECE, 16), PIECE)

    def rs_copy(slot, k, d):
        to = (x + d) % 4
        return pltpu.make_async_remote_copy(
            src_ref=part.at[slot, piece(k, to * CHUNK)], dst_ref=rs_buf.at[slot, d - 1, piece(k)],
            send_sem=rs_send.at[slot, k, d - 1], recv_sem=rs_recv.at[slot, k, d - 1],
            device_id=at_x(d), device_id_type=MESH,
        )

    def z_copy(slot, k):
        return pltpu.make_async_remote_copy(
            src_ref=z_own.at[slot, piece(k)], dst_ref=z_buf.at[slot, piece(k)],
            send_sem=z_send.at[slot, k], recv_sem=z_recv.at[slot, k],
            device_id=twin, device_id_type=MESH,
        )

    def ag_copy(slot, k, d):
        return pltpu.make_async_remote_copy(
            src_ref=gathered.at[slot, x, piece(k)], dst_ref=gathered.at[slot, x, piece(k)],
            send_sem=ag_send.at[slot, k, d - 1], recv_sem=ag_recv.at[slot, k, d - 1],
            device_id=at_x(d), device_id_type=MESH,
        )

    def scatter(slot):
        for a, terms in enumerate(TAPS):
            total = 0.0
            for t, q, p in terms:
                block = (slice(q * K, (q + 1) * K), lanes(p))
                total += acc[slot, t, *block] + acc[slot, t + 1, *block]
            part[slot, a * K : (a + 1) * K] = (factor * total).astype(bf16)
        for k in range(PIECES):
            for d in (2, 1, 3):
                rs_copy(slot, k, d).start()

    def exchange(slot, k):
        for d in (1, 3, 2):
            rs_copy(slot, k, d).wait_recv()
        total = part[slot, piece(k, x * CHUNK)].astype(f32)
        for d in (1, 2, 3):
            total += rs_buf[slot, d - 1, piece(k)].astype(f32)
        z_own[slot, piece(k)] = total.astype(bf16)
        z_copy(slot, k).start()

    def gather(slot, k):
        z_copy(slot, k).wait_recv()
        total = z_own[slot, piece(k)].astype(f32) + z_buf[slot, piece(k)].astype(f32)
        gathered[slot, x, piece(k)] = total.astype(bf16)
        for d in (2, 1, 3):
            ag_copy(slot, k, d).start()

    def finish(slot):
        for k in range(PIECES):
            for d in (1, 3, 2):
                ag_copy(slot, k, d).wait_recv()
        summed[slot] = gathered[slot]

    lax.fori_loop(0, IMAGES // 2 - 1, second_pass, 0)
    arrived(IMAGES - 2)
    add_grad(1, xs1, top, IMAGES - 2, 1)
    step_back(IMAGES - 2, 0)
    arrived(IMAGES - 1)
    add_grad(1, xs1, top, IMAGES - 1, 1)
    scatter(1)
    step_back(IMAGES - 1, 1)
    add_grad(0, xs0, a1, IMAGES - 4, 4)
    scatter(0)
    order = [(slot, k) for slot in (1, 0) for k in range(PIECES)]
    for n in range(len(order) + PIECES):
        if n < len(order):
            exchange(*order[n])
        if n >= PIECES:
            gather(*order[n - PIECES])
    finish(1)
    finish(0)

    for slot in range(2):
        for k in range(PIECES):
            for d in (1, 2, 3):
                rs_copy(slot, k, d).wait_send()
                ag_copy(slot, k, d).wait_send()
            z_copy(slot, k).wait_send()

    def drain(i, carry):
        @pl.when(has_below)
        def _():
            send_copy(i).wait_send()

        return carry

    lax.fori_loop(0, IMAGES, drain, 0)


def deliver(low_v, sum_v, low_out, grad_out, grad_v, low_sem, grad_sem):
    def low_copy(i):
        return pltpu.make_async_copy(low_v.at[i], low_out.at[i], low_sem.at[i])

    def grad_copy(slot):
        return pltpu.make_async_copy(grad_v.at[slot], grad_out.at[slot], grad_sem.at[slot])

    for i in range(IMAGES):
        low_copy(i).start()
    for slot in range(2):
        grad_v[slot] = sum_v[slot].astype(f32)
        grad_copy(slot).start()
    for slot in range(2):
        grad_copy(slot).wait()
    for i in range(IMAGES):
        low_copy(i).wait()


def body(u_c, lam_c, weights):
    image = (IMAGES, PAIRS, 2, W, C)
    pair = (IMAGES, PAIRS, W, 2 * C)
    patch = (PAIRS + 1, W, 2 * K)
    wide = (3, 2 * K, 2 * C)
    vmem, dma = pltpu.VMEM, pltpu.SemaphoreType.DMA
    low, grad = pl.pallas_call(
        kernel,
        out_shape=(pltpu.VMEM(image, bf16), pltpu.VMEM((2, 4, CHUNK, C), bf16)),
        in_specs=[pl.BlockSpec(memory_space=pl.ANY)] * 3,
        out_specs=(pl.BlockSpec(memory_space=vmem),) * 2,
        scratch_shapes=[
            vmem(image, bf16), vmem(image, bf16), vmem((2, 3, 3, C, C), bf16),
            vmem((IMAGES,) + patch, bf16), vmem((IMAGES,) + patch, bf16), vmem((2,) + patch, bf16), vmem(patch, bf16),
            vmem((2, PAIRS, W, 2 * C), bf16), vmem(pair, bf16),
            vmem(pair, bf16), vmem(pair, bf16), vmem(pair, bf16),
            vmem((2, 3, 2 * K, 2 * C), f32),
            vmem(wide, bf16), vmem(wide, bf16), vmem(wide, bf16),
            vmem((2, 9 * C, C), bf16), vmem((2, 3, CHUNK, C), bf16),
            vmem((2, CHUNK, C), bf16), vmem((2, CHUNK, C), bf16),
            vmem((2, 4, CHUNK, C), bf16),
            dma((IMAGES,)), dma((IMAGES,)), dma((2,)),
            dma((IMAGES,)), dma((IMAGES,)),
            dma((2, PIECES, 3)), dma((2, PIECES, 3)), dma((2, PIECES)), dma((2, PIECES)),
            dma((2, PIECES, 3)), dma((2, PIECES, 3)),
        ],
        compiler_params=pltpu.CompilerParams(
            collective_id=0, has_side_effects=True, vmem_limit_bytes=52 * 2**20
        ),
        cost_estimate=pl.CostEstimate(flops=15 * 10**9, bytes_accessed=10**7, transcendentals=2 * 10**6),
        name="relax",
    )(u_c.reshape(image), lam_c.reshape(image), weights)
    low, grad = pl.pallas_call(
        deliver,
        out_shape=(
            jax.ShapeDtypeStruct(image, bf16),
            jax.ShapeDtypeStruct((2, 4, CHUNK, C), f32),
        ),
        in_specs=[pl.BlockSpec(memory_space=vmem)] * 2,
        out_specs=(pl.BlockSpec(memory_space=pl.ANY),) * 2,
        scratch_shapes=[vmem((2, 4, CHUNK, C), f32), dma((IMAGES,)), dma((2,))],
        compiler_params=pltpu.CompilerParams(vmem_limit_bytes=8 * 2**20),
        name="deliver",
    )(low, grad)
    return low.reshape(1, IMAGES, 2 * PAIRS, W, C), grad.reshape(2, 3, 3, C, C)


def solution(mesh):
    placed = (
        P("layer", "batch", None, None, None),
        P("layer", "batch", None, None, None),
        P("layer", None, None, None, None),
    )
    return jax.shard_map(
        body,
        mesh=mesh,
        in_specs=placed,
        out_specs=(P("layer", "batch", None, None, None), P("layer", None, None, None, None)),
        check_vma=False,
    )
```

```python
import functools

import jax
import jax.numpy as jnp
from jax import lax
from jax.experimental import pallas as pl
from jax.experimental.pallas import tpu as pltpu
from jax.sharding import PartitionSpec as P

f32 = jnp.float32
bf16 = jnp.bfloat16
MESH = pl.DeviceIdType.MESH
IMAGES = 8
PAIRS = 16
ROWS = 8
CHUNKS = tuple(range(0, PAIRS, ROWS))
W = 32
C = 128
K = 3 * C
CHUNK = 288
PIECES = 2
PIECE = CHUNK // PIECES
TAPS = (((0, 0, 0), (0, 1, 1)), ((0, 1, 0), (1, 0, 1)), ((1, 0, 0), (1, 1, 1)))
depth_step = 0.5


def silu_parts(v):
    t = 0.5 * jnp.tanh(0.5 * v) + 0.5
    return v * t, depth_step * (t * (1.0 + v * (1.0 - t)))


def put_rows(x_ref, at, parity, value):
    column = lax.broadcasted_iota(jnp.int32, value.shape, 1)
    before = jnp.where(column == 0, 0.0, pltpu.roll(value, 1, 1))
    after = jnp.where(column == W - 1, 0.0, pltpu.roll(value, W - 1, 1))
    first = at if parity == 0 else at + 1
    lane = K if parity == 0 else 0
    for b, part in enumerate((before, value, after)):
        x_ref[first : first + ROWS, :, lane + b * C : lane + (b + 1) * C] = part.astype(bf16)


def clear_edges(x_ref):
    x_ref[0, :, 0:K] = jnp.zeros((W, K), bf16)
    x_ref[PAIRS, :, K : 2 * K] = jnp.zeros((W, K), bf16)


def conv(x_ref, w_ref, at):
    n = ROWS // 2 * W
    d = x_ref[at : at + ROWS].reshape(ROWS // 2, 2, W, 2 * K)
    later = x_ref[at + 1 : at + ROWS + 1].reshape(ROWS // 2, 2, W, 2 * K)
    d0, d1, d2 = (v.reshape(n, 2 * K) for v in (d[:, 0], d[:, 1], later[:, 1]))
    shared = jnp.dot(d1, w_ref[1], preferred_element_type=f32)
    upper = shared + jnp.dot(d0 - d1, w_ref[0], preferred_element_type=f32)
    lower = shared + jnp.dot(d2 - d1, w_ref[2], preferred_element_type=f32)
    shape = (ROWS // 2, W, 2 * C)
    y = jnp.stack([upper.reshape(shape), lower.reshape(shape)], axis=1).reshape(ROWS, W, 2 * C)
    return y[:, :, :C], y[:, :, C:]


def fill_weights(dst, src, layer, transposed):
    for t in range(2):
        for q in range(2):
            for p in range(2):
                a = 2 * t + q - p
                for b in range(3):
                    rows = slice(q * K + b * C, q * K + (b + 1) * C)
                    cols = slice(p * C, (p + 1) * C)
                    if not 0 <= a <= 2:
                        dst[2 * t, rows, cols] = jnp.zeros((C, C), bf16)
                    elif transposed:
                        dst[2 * t, rows, cols] = src[layer, 2 - a, 2 - b].T
                    else:
                        dst[2 * t, rows, cols] = src[layer, a, b]
    dst[1] = dst[0] + dst[2]


def kernel(
    u_hbm, lam_hbm, w_hbm, low_v, summed,
    u_v, lam_v, w_v, xs0, xs1, xq, xr, g0, g1, bottom, top, a1, acc,
    wf, wt0, wt1, part, rs_buf, z_own, z_buf, gathered,
    u_sem, lam_sem, w_sem, send_sem, recv_sem,
    rs_send, rs_recv, z_send, z_recv, ag_send, ag_recv,
):
    layer = lax.axis_index("layer")
    batch = lax.axis_index("batch")
    x, zh = batch // 2, batch % 2
    below, above = jnp.maximum(layer - 1, 0), jnp.minimum(layer + 1, 31)
    has_below, has_above = layer > 0, layer < 31
    over_links = layer % 2 == 1

    def at_x(d):
        return (layer, ((x + d) % 4) * 2 + zh)

    twin = (layer, x * 2 + 1 - zh)

    def w_copy(slot):
        return pltpu.make_async_copy(w_hbm.at[slot], w_v.at[slot], w_sem.at[slot])

    def u_copy(i):
        return pltpu.make_async_copy(u_hbm.at[i], u_v.at[i], u_sem.at[i])

    def lam_copy(i):
        return pltpu.make_async_copy(lam_hbm.at[i], lam_v.at[i], lam_sem.at[i])

    u_copy(0).start()
    w_copy(0).start()
    lam_copy(0).start()
    w_copy(1).start()
    barrier = pltpu.get_barrier_semaphore()

    @pl.when(has_below)
    def _():
        pl.semaphore_signal(barrier, inc=1, device_id=(below, batch), device_id_type=MESH)

    @pl.when(has_above)
    def _():
        pl.semaphore_signal(barrier, inc=1, device_id=(above, batch), device_id_type=MESH)

    for d in (1, 2, 3):
        pl.semaphore_signal(barrier, inc=1, device_id=at_x(d), device_id_type=MESH)
    pl.semaphore_signal(barrier, inc=1, device_id=twin, device_id_type=MESH)

    clear_edges(xq.at[0])
    clear_edges(xq.at[1])
    clear_edges(xr)
    acc[...] = jnp.zeros_like(acc)

    def clear(i, carry):
        clear_edges(xs0.at[i])
        clear_edges(xs1.at[i])
        return carry

    lax.fori_loop(0, IMAGES, clear, 0)
    def send_copy(i):
        return pltpu.make_async_remote_copy(
            src_ref=bottom.at[i], dst_ref=top.at[i], send_sem=send_sem.at[i], recv_sem=recv_sem.at[i],
            device_id=(below, batch), device_id_type=MESH,
        )

    def lanes(p):
        return slice(p * C, (p + 1) * C)

    def load(i):
        u_copy(i).wait()
        lam_copy(i).wait()

    def open_state(i, slot, at):
        rows = slice(at, at + ROWS)
        for p in range(2):
            s, g = silu_parts(u_v[i, rows, p].astype(f32))
            put_rows(xs0.at[i], at, p, s)
            g0[slot, rows, :, lanes(p)] = g.astype(bf16)

    def open_adjoint(i, slot, at):
        for p in range(2):
            put_rows(xq.at[slot], at, p, lam_v[i, at : at + ROWS, p].astype(f32))

    def first_pass(i, carry):
        now, then = lax.rem(i, 2), lax.rem(i + 1, 2)
        ahead = jnp.minimum(i + 1, IMAGES - 1)

        @pl.when(i < IMAGES - 1)
        def _():
            load(ahead)

        for at in CHUNKS:
            rows = slice(at, at + ROWS)
            for p, y in enumerate(conv(xs0.at[i], wf, at)):
                moved = (u_v[i, rows, p].astype(f32) + depth_step * y).astype(bf16).astype(f32)
                s, g = silu_parts(moved)
                put_rows(xs1.at[i], at, p, s)
                g1[i, rows, :, lanes(p)] = g.astype(bf16)
        for at in CHUNKS:
            rows = slice(at, at + ROWS)
            for p, y in enumerate(conv(xq.at[now], wt1, at)):
                g = g1[i, rows, :, lanes(p)].astype(f32)
                put_rows(xr, at, p, (lam_v[i, rows, p].astype(f32) + g * y).astype(bf16).astype(f32))
            open_adjoint(ahead, then, at)
        for at in CHUNKS:
            rows = slice(at, at + ROWS)
            for p, y in enumerate(conv(xr, wt0, at)):
                first, lane = (at, K + C) if p == 0 else (at + 1, C)
                centre = xr[first : first + ROWS, :, lane : lane + C].astype(f32)
                g = g0[now, rows, :, lanes(p)].astype(f32)
                bottom[i, rows, :, lanes(p)] = (centre + g * y).astype(bf16)
            open_state(ahead, then, at)

        @pl.when(has_below)
        def _():
            send_copy(i).start()

        @pl.when(jnp.logical_not(has_above))
        def _():
            for p in range(2):
                top[i, :, :, lanes(p)] = lam_v[i, :, p]

        return carry

    u_copy(0).wait()
    for at in CHUNKS:
        open_state(0, 0, at)
    lam_copy(0).wait()
    w_copy(0).wait()
    w_copy(1).wait()
    for i in range(1, IMAGES):
        u_copy(i).start()
        lam_copy(i).start()
    fill_weights(wf, w_v, 0, False)
    for at in CHUNKS:
        open_adjoint(0, 0, at)
    fill_weights(wt1, w_v, 1, True)
    fill_weights(wt0, w_v, 0, True)
    peers = 4 + jnp.where(has_below, 1, 0) + jnp.where(has_above, 1, 0)
    pl.semaphore_wait(barrier, peers)

    lax.fori_loop(0, IMAGES, first_pass, 0)

    def add_grad(slot, xs, adj, i, count):
        n = count * PAIRS // 2 * W
        r = adj[pl.ds(i, count)].reshape(count, PAIRS // 2, 2, W, 2 * C)
        d = xs[pl.ds(i, count), 0:PAIRS].reshape(count, PAIRS // 2, 2, W, 2 * K)
        later = xs[pl.ds(i, count), 1 : PAIRS + 1].reshape(count, PAIRS // 2, 2, W, 2 * K)
        r0, r1 = r[:, :, 0], r[:, :, 1]
        d0, d1, d2 = d[:, :, 0], d[:, :, 1], later[:, :, 1]
        for t, (left, right) in enumerate(((d0 - d1, r0), (d1, r0 + r1), (d2 - d1, r1))):
            acc[slot, t] += lax.dot_general(
                left.reshape(n, 2 * K), right.reshape(n, 2 * C),
                (((0,), (0,)), ((), ())), preferred_element_type=f32,
            )

    def step_back(i, slot):
        for at in CHUNKS:
            rows = slice(at, at + ROWS)
            for p in range(2):
                put_rows(xq.at[slot], at, p, top[i, rows, :, lanes(p)].astype(f32))
        for at in CHUNKS:
            rows = slice(at, at + ROWS)
            for p, y in enumerate(conv(xq.at[slot], wt1, at)):
                moved = top[i, rows, :, lanes(p)].astype(f32) + g1[i, rows, :, lanes(p)].astype(f32) * y
                a1[i, rows, :, lanes(p)] = moved.astype(bf16)
                low_v[i, rows, p] = moved.astype(bf16)

    def arrived(i):
        @pl.when(has_above)
        def _():
            send_copy(i).wait_recv()

    def second_pass(j, carry):
        for slot in range(2):
            arrived(2 * j + slot)
            step_back(2 * j + slot, slot)
        add_grad(1, xs1, top, 2 * j, 2)

        @pl.when(jnp.logical_or(j < 2, over_links))
        def _():
            add_grad(0, xs0, a1, 2 * j, 2)

        return carry

    factor = depth_step / (IMAGES * 8)

    def piece(k, first=0):
        return pl.ds(pl.multiple_of(first + k * PIECE, 16), PIECE)

    def rs_copy(slot, k, d):
        to = (x + d) % 4
        return pltpu.make_async_remote_copy(
            src_ref=part.at[slot, piece(k, to * CHUNK)], dst_ref=rs_buf.at[slot, d - 1, piece(k)],
            send_sem=rs_send.at[slot, k, d - 1], recv_sem=rs_recv.at[slot, k, d - 1],
            device_id=at_x(d), device_id_type=MESH,
        )

    def z_copy(slot, k):
        return pltpu.make_async_remote_copy(
            src_ref=z_own.at[slot, piece(k)], dst_ref=z_buf.at[slot, piece(k)],
            send_sem=z_send.at[slot, k], recv_sem=z_recv.at[slot, k],
            device_id=twin, device_id_type=MESH,
        )

    def ag_copy(slot, k, d):
        return pltpu.make_async_remote_copy(
            src_ref=gathered.at[slot, x, piece(k)], dst_ref=gathered.at[slot, x, piece(k)],
            send_sem=ag_send.at[slot, k, d - 1], recv_sem=ag_recv.at[slot, k, d - 1],
            device_id=at_x(d), device_id_type=MESH,
        )

    def scatter(slot):
        for a, terms in enumerate(TAPS):
            total = 0.0
            for t, q, p in terms:
                block = (slice(q * K, (q + 1) * K), lanes(p))
                total += acc[slot, t, *block] + acc[slot, t + 1, *block]
            part[slot, a * K : (a + 1) * K] = (factor * total).astype(bf16)
        for k in range(PIECES):
            for d in (2, 1, 3):
                rs_copy(slot, k, d).start()

    def exchange(slot, k):
        for d in (1, 3, 2):
            rs_copy(slot, k, d).wait_recv()
        total = part[slot, piece(k, x * CHUNK)].astype(f32)
        for d in (1, 2, 3):
            total += rs_buf[slot, d - 1, piece(k)].astype(f32)
        z_own[slot, piece(k)] = total.astype(bf16)
        z_copy(slot, k).start()

    def gather(slot, k):
        z_copy(slot, k).wait_recv()
        total = z_own[slot, piece(k)].astype(f32) + z_buf[slot, piece(k)].astype(f32)
        gathered[slot, x, piece(k)] = total.astype(bf16)
        for d in (2, 1, 3):
            ag_copy(slot, k, d).start()

    def finish(slot):
        for k in range(PIECES):
            for d in (1, 3, 2):
                ag_copy(slot, k, d).wait_recv()
        summed[slot] = gathered[slot]

    lax.fori_loop(0, IMAGES // 2 - 1, second_pass, 0)
    arrived(IMAGES - 2)
    add_grad(1, xs1, top, IMAGES - 2, 1)
    step_back(IMAGES - 2, 0)

    @pl.when(over_links)
    def _():
        add_grad(0, xs0, a1, IMAGES - 2, 1)

    arrived(IMAGES - 1)
    add_grad(1, xs1, top, IMAGES - 1, 1)
    scatter(1)
    step_back(IMAGES - 1, 1)

    @pl.when(over_links)
    def _():
        add_grad(0, xs0, a1, IMAGES - 1, 1)

    @pl.when(jnp.logical_not(over_links))
    def _():
        add_grad(0, xs0, a1, IMAGES - 4, 4)

    scatter(0)
    order = [(slot, k) for slot in (1, 0) for k in range(PIECES)]
    for n in range(len(order) + PIECES):
        if n < len(order):
            exchange(*order[n])
        if n >= PIECES:
            gather(*order[n - PIECES])
    finish(1)
    finish(0)

    for slot in range(2):
        for k in range(PIECES):
            for d in (1, 2, 3):
                rs_copy(slot, k, d).wait_send()
                ag_copy(slot, k, d).wait_send()
            z_copy(slot, k).wait_send()

    def drain(i, carry):
        @pl.when(has_below)
        def _():
            send_copy(i).wait_send()

        return carry

    lax.fori_loop(0, IMAGES, drain, 0)


def deliver(low_v, sum_v, low_out, grad_out, grad_v, low_sem, grad_sem):
    def low_copy(i):
        return pltpu.make_async_copy(low_v.at[i], low_out.at[i], low_sem.at[i])

    def grad_copy(slot):
        return pltpu.make_async_copy(grad_v.at[slot], grad_out.at[slot], grad_sem.at[slot])

    for i in range(IMAGES):
        low_copy(i).start()
    for slot in range(2):
        grad_v[slot] = sum_v[slot].astype(f32)
        grad_copy(slot).start()
    for slot in range(2):
        grad_copy(slot).wait()
    for i in range(IMAGES):
        low_copy(i).wait()


def body(u_c, lam_c, weights):
    image = (IMAGES, PAIRS, 2, W, C)
    pair = (IMAGES, PAIRS, W, 2 * C)
    patch = (PAIRS + 1, W, 2 * K)
    wide = (3, 2 * K, 2 * C)
    vmem, dma = pltpu.VMEM, pltpu.SemaphoreType.DMA
    low, grad = pl.pallas_call(
        kernel,
        out_shape=(pltpu.VMEM(image, bf16), pltpu.VMEM((2, 4, CHUNK, C), bf16)),
        in_specs=[pl.BlockSpec(memory_space=pl.ANY)] * 3,
        out_specs=(pl.BlockSpec(memory_space=vmem),) * 2,
        scratch_shapes=[
            vmem(image, bf16), vmem(image, bf16), vmem((2, 3, 3, C, C), bf16),
            vmem((IMAGES,) + patch, bf16), vmem((IMAGES,) + patch, bf16), vmem((2,) + patch, bf16), vmem(patch, bf16),
            vmem((2, PAIRS, W, 2 * C), bf16), vmem(pair, bf16),
            vmem(pair, bf16), vmem(pair, bf16), vmem(pair, bf16),
            vmem((2, 3, 2 * K, 2 * C), f32),
            vmem(wide, bf16), vmem(wide, bf16), vmem(wide, bf16),
            vmem((2, 9 * C, C), bf16), vmem((2, 3, CHUNK, C), bf16),
            vmem((2, CHUNK, C), bf16), vmem((2, CHUNK, C), bf16),
            vmem((2, 4, CHUNK, C), bf16),
            dma((IMAGES,)), dma((IMAGES,)), dma((2,)),
            dma((IMAGES,)), dma((IMAGES,)),
            dma((2, PIECES, 3)), dma((2, PIECES, 3)), dma((2, PIECES)), dma((2, PIECES)),
            dma((2, PIECES, 3)), dma((2, PIECES, 3)),
        ],
        compiler_params=pltpu.CompilerParams(
            collective_id=0, has_side_effects=True, vmem_limit_bytes=52 * 2**20
        ),
        cost_estimate=pl.CostEstimate(flops=15 * 10**9, bytes_accessed=10**7, transcendentals=2 * 10**6),
        name="relax",
    )(u_c.reshape(image), lam_c.reshape(image), weights)
    low, grad = pl.pallas_call(
        deliver,
        out_shape=(
            jax.ShapeDtypeStruct(image, bf16),
            jax.ShapeDtypeStruct((2, 4, CHUNK, C), f32),
        ),
        in_specs=[pl.BlockSpec(memory_space=vmem)] * 2,
        out_specs=(pl.BlockSpec(memory_space=pl.ANY),) * 2,
        scratch_shapes=[vmem((2, 4, CHUNK, C), f32), dma((IMAGES,)), dma((2,))],
        compiler_params=pltpu.CompilerParams(vmem_limit_bytes=8 * 2**20),
        name="deliver",
    )(low, grad)
    return low.reshape(1, IMAGES, 2 * PAIRS, W, C), grad.reshape(2, 3, 3, C, C)


def solution(mesh):
    placed = (
        P("layer", "batch", None, None, None),
        P("layer", "batch", None, None, None),
        P("layer", None, None, None, None),
    )
    return jax.shard_map(
        body,
        mesh=mesh,
        in_specs=placed,
        out_specs=(P("layer", "batch", None, None, None), P("layer", None, None, None, None)),
        check_vma=False,
    )
```

```python
import functools

import jax
import jax.numpy as jnp
from jax import lax
from jax.experimental import pallas as pl
from jax.experimental.pallas import tpu as pltpu
from jax.sharding import PartitionSpec as P

f32 = jnp.float32
bf16 = jnp.bfloat16
MESH = pl.DeviceIdType.MESH
IMAGES = 8
PAIRS = 16
ROWS = 8
CHUNKS = tuple(range(0, PAIRS, ROWS))
W = 32
C = 128
K = 3 * C
CHUNK = 288
PIECES = 2
PIECE = CHUNK // PIECES
TAPS = (((0, 0, 0), (0, 1, 1)), ((0, 1, 0), (1, 0, 1)), ((1, 0, 0), (1, 1, 1)))
depth_step = 0.5


def silu_parts(v):
    t = 0.5 * jnp.tanh(0.5 * v) + 0.5
    return v * t, depth_step * (t * (1.0 + v * (1.0 - t)))


def put_rows(x_ref, at, parity, value):
    column = lax.broadcasted_iota(jnp.int32, value.shape, 1)
    before = jnp.where(column == 0, 0.0, pltpu.roll(value, 1, 1))
    after = jnp.where(column == W - 1, 0.0, pltpu.roll(value, W - 1, 1))
    first = at if parity == 0 else at + 1
    lane = K if parity == 0 else 0
    for b, part in enumerate((before, value, after)):
        x_ref[first : first + ROWS, :, lane + b * C : lane + (b + 1) * C] = part.astype(bf16)


def clear_edges(x_ref):
    x_ref[0, :, 0:K] = jnp.zeros((W, K), bf16)
    x_ref[PAIRS, :, K : 2 * K] = jnp.zeros((W, K), bf16)


def conv(x_ref, w_ref, at):
    n = ROWS // 2 * W
    d = x_ref[at : at + ROWS].reshape(ROWS // 2, 2, W, 2 * K)
    later = x_ref[at + 1 : at + ROWS + 1].reshape(ROWS // 2, 2, W, 2 * K)
    d0, d1, d2 = (v.reshape(n, 2 * K) for v in (d[:, 0], d[:, 1], later[:, 1]))
    shared = jnp.dot(d1, w_ref[1], preferred_element_type=f32)
    upper = shared + jnp.dot(d0 - d1, w_ref[0], preferred_element_type=f32)
    lower = shared + jnp.dot(d2 - d1, w_ref[2], preferred_element_type=f32)
    shape = (ROWS // 2, W, 2 * C)
    y = jnp.stack([upper.reshape(shape), lower.reshape(shape)], axis=1).reshape(ROWS, W, 2 * C)
    return y[:, :, :C], y[:, :, C:]


def fill_weights(dst, src, layer, transposed):
    for t in range(2):
        for q in range(2):
            for p in range(2):
                a = 2 * t + q - p
                for b in range(3):
                    rows = slice(q * K + b * C, q * K + (b + 1) * C)
                    cols = slice(p * C, (p + 1) * C)
                    if not 0 <= a <= 2:
                        dst[2 * t, rows, cols] = jnp.zeros((C, C), bf16)
                    elif transposed:
                        dst[2 * t, rows, cols] = src[layer, 2 - a, 2 - b].T
                    else:
                        dst[2 * t, rows, cols] = src[layer, a, b]
    dst[1] = dst[0] + dst[2]


def kernel(
    u_hbm, lam_hbm, w_hbm, low_v, summed,
    u_v, lam_v, w_v, xs0, xs1, xq, xr, g0, g1, bottom, top, a1, acc,
    wf, wt0, wt1, part, rs_buf, z_own, z_buf, gathered,
    u_sem, lam_sem, w_sem, send_sem, recv_sem,
    rs_send, rs_recv, z_send, z_recv, ag_send, ag_recv,
):
    layer = lax.axis_index("layer")
    batch = lax.axis_index("batch")
    x, zh = batch // 2, batch % 2
    below, above = jnp.maximum(layer - 1, 0), jnp.minimum(layer + 1, 31)
    has_below, has_above = layer > 0, layer < 31
    over_links = layer % 2 == 1

    def at_x(d):
        return (layer, ((x + d) % 4) * 2 + zh)

    twin = (layer, x * 2 + 1 - zh)

    def w_copy(slot):
        return pltpu.make_async_copy(w_hbm.at[slot], w_v.at[slot], w_sem.at[slot])

    def u_copy(i):
        return pltpu.make_async_copy(u_hbm.at[i], u_v.at[i], u_sem.at[i])

    def lam_copy(i):
        return pltpu.make_async_copy(lam_hbm.at[i], lam_v.at[i], lam_sem.at[i])

    u_copy(0).start()
    w_copy(0).start()
    lam_copy(0).start()
    w_copy(1).start()
    barrier = pltpu.get_barrier_semaphore()

    @pl.when(has_below)
    def _():
        pl.semaphore_signal(barrier, inc=1, device_id=(below, batch), device_id_type=MESH)

    @pl.when(has_above)
    def _():
        pl.semaphore_signal(barrier, inc=1, device_id=(above, batch), device_id_type=MESH)

    for d in (1, 2, 3):
        pl.semaphore_signal(barrier, inc=1, device_id=at_x(d), device_id_type=MESH)
    pl.semaphore_signal(barrier, inc=1, device_id=twin, device_id_type=MESH)

    clear_edges(xq.at[0])
    clear_edges(xq.at[1])
    clear_edges(xr)
    acc[...] = jnp.zeros_like(acc)

    def clear(i, carry):
        clear_edges(xs0.at[i])
        clear_edges(xs1.at[i])
        return carry

    lax.fori_loop(0, IMAGES, clear, 0)
    def send_copy(i):
        return pltpu.make_async_remote_copy(
            src_ref=bottom.at[i], dst_ref=top.at[i], send_sem=send_sem.at[i], recv_sem=recv_sem.at[i],
            device_id=(below, batch), device_id_type=MESH,
        )

    def lanes(p):
        return slice(p * C, (p + 1) * C)

    def load(i):
        u_copy(i).wait()
        lam_copy(i).wait()

    def open_state(i, slot, at):
        rows = slice(at, at + ROWS)
        for p in range(2):
            s, g = silu_parts(u_v[i, rows, p].astype(f32))
            put_rows(xs0.at[i], at, p, s)
            g0[slot, rows, :, lanes(p)] = g.astype(bf16)

    def open_adjoint(i, slot, at):
        for p in range(2):
            put_rows(xq.at[slot], at, p, lam_v[i, at : at + ROWS, p].astype(f32))

    def first_pass(i, carry):
        now, then = lax.rem(i, 2), lax.rem(i + 1, 2)
        ahead = jnp.minimum(i + 1, IMAGES - 1)

        @pl.when(i < IMAGES - 1)
        def _():
            load(ahead)

        for at in CHUNKS:
            rows = slice(at, at + ROWS)
            for p, y in enumerate(conv(xs0.at[i], wf, at)):
                moved = (u_v[i, rows, p].astype(f32) + depth_step * y).astype(bf16).astype(f32)
                s, g = silu_parts(moved)
                put_rows(xs1.at[i], at, p, s)
                g1[i, rows, :, lanes(p)] = g.astype(bf16)
        for at in CHUNKS:
            rows = slice(at, at + ROWS)
            for p, y in enumerate(conv(xq.at[now], wt1, at)):
                g = g1[i, rows, :, lanes(p)].astype(f32)
                put_rows(xr, at, p, (lam_v[i, rows, p].astype(f32) + g * y).astype(bf16).astype(f32))
            open_adjoint(ahead, then, at)
        for at in CHUNKS:
            rows = slice(at, at + ROWS)
            for p, y in enumerate(conv(xr, wt0, at)):
                first, lane = (at, K + C) if p == 0 else (at + 1, C)
                centre = xr[first : first + ROWS, :, lane : lane + C].astype(f32)
                g = g0[now, rows, :, lanes(p)].astype(f32)
                bottom[i, rows, :, lanes(p)] = (centre + g * y).astype(bf16)
            open_state(ahead, then, at)

        @pl.when(has_below)
        def _():
            send_copy(i).start()

        @pl.when(jnp.logical_not(has_above))
        def _():
            for p in range(2):
                top[i, :, :, lanes(p)] = lam_v[i, :, p]

        return carry

    u_copy(0).wait()
    for at in CHUNKS:
        open_state(0, 0, at)
    lam_copy(0).wait()
    w_copy(0).wait()
    w_copy(1).wait()
    for i in range(1, IMAGES):
        u_copy(i).start()
        lam_copy(i).start()
    fill_weights(wf, w_v, 0, False)
    for at in CHUNKS:
        open_adjoint(0, 0, at)
    fill_weights(wt1, w_v, 1, True)
    fill_weights(wt0, w_v, 0, True)
    peers = 4 + jnp.where(has_below, 1, 0) + jnp.where(has_above, 1, 0)
    pl.semaphore_wait(barrier, peers)

    lax.fori_loop(0, IMAGES, first_pass, 0)

    def add_grad(slot, xs, adj, i, count):
        n = count * PAIRS // 2 * W
        r = adj[pl.ds(i, count)].reshape(count, PAIRS // 2, 2, W, 2 * C)
        d = xs[pl.ds(i, count), 0:PAIRS].reshape(count, PAIRS // 2, 2, W, 2 * K)
        later = xs[pl.ds(i, count), 1 : PAIRS + 1].reshape(count, PAIRS // 2, 2, W, 2 * K)
        r0, r1 = r[:, :, 0], r[:, :, 1]
        d0, d1, d2 = d[:, :, 0], d[:, :, 1], later[:, :, 1]
        for t, (left, right) in enumerate(((d0 - d1, r0), (d1, r0 + r1), (d2 - d1, r1))):
            acc[slot, t] += lax.dot_general(
                left.reshape(n, 2 * K), right.reshape(n, 2 * C),
                (((0,), (0,)), ((), ())), preferred_element_type=f32,
            )

    def step_back(i, slot):
        for at in CHUNKS:
            rows = slice(at, at + ROWS)
            for p in range(2):
                put_rows(xq.at[slot], at, p, top[i, rows, :, lanes(p)].astype(f32))
        for at in CHUNKS:
            rows = slice(at, at + ROWS)
            for p, y in enumerate(conv(xq.at[slot], wt1, at)):
                moved = top[i, rows, :, lanes(p)].astype(f32) + g1[i, rows, :, lanes(p)].astype(f32) * y
                a1[i, rows, :, lanes(p)] = moved.astype(bf16)
                low_v[i, rows, p] = moved.astype(bf16)

    def arrived(i):
        @pl.when(has_above)
        def _():
            send_copy(i).wait_recv()

    def second_pass(j, carry):
        for slot in range(2):
            arrived(2 * j + slot)
            step_back(2 * j + slot, slot)
        add_grad(1, xs1, top, 2 * j, 2)

        @pl.when(jnp.logical_or(j < 2, over_links))
        def _():
            add_grad(0, xs0, a1, 2 * j, 2)

        return carry

    factor = depth_step / (IMAGES * 8)

    def piece(k, first=0):
        return pl.ds(pl.multiple_of(first + k * PIECE, 16), PIECE)

    def rs_copy(slot, k, d):
        to = (x + d) % 4
        return pltpu.make_async_remote_copy(
            src_ref=part.at[slot, piece(k, to * CHUNK)], dst_ref=rs_buf.at[slot, d - 1, piece(k)],
            send_sem=rs_send.at[slot, k, d - 1], recv_sem=rs_recv.at[slot, k, d - 1],
            device_id=at_x(d), device_id_type=MESH,
        )

    def z_copy(slot, k):
        return pltpu.make_async_remote_copy(
            src_ref=z_own.at[slot, piece(k)], dst_ref=z_buf.at[slot, piece(k)],
            send_sem=z_send.at[slot, k], recv_sem=z_recv.at[slot, k],
            device_id=twin, device_id_type=MESH,
        )

    def ag_copy(slot, k, d):
        return pltpu.make_async_remote_copy(
            src_ref=gathered.at[slot, x, piece(k)], dst_ref=gathered.at[slot, x, piece(k)],
            send_sem=ag_send.at[slot, k, d - 1], recv_sem=ag_recv.at[slot, k, d - 1],
            device_id=at_x(d), device_id_type=MESH,
        )

    def scatter(slot):
        for a, terms in enumerate(TAPS):
            total = 0.0
            for t, q, p in terms:
                block = (slice(q * K, (q + 1) * K), lanes(p))
                total += acc[slot, t, *block] + acc[slot, t + 1, *block]
            part[slot, a * K : (a + 1) * K] = (factor * total).astype(bf16)
        for k in range(PIECES):
            for d in (2, 1, 3):
                rs_copy(slot, k, d).start()

    def exchange(slot, k):
        for d in (1, 3, 2):
            rs_copy(slot, k, d).wait_recv()
        total = part[slot, piece(k, x * CHUNK)].astype(f32)
        for d in (1, 2, 3):
            total += rs_buf[slot, d - 1, piece(k)].astype(f32)
        z_own[slot, piece(k)] = total.astype(bf16)
        z_copy(slot, k).start()

    def gather(slot, k):
        z_copy(slot, k).wait_recv()
        total = z_own[slot, piece(k)].astype(f32) + z_buf[slot, piece(k)].astype(f32)
        gathered[slot, x, piece(k)] = total.astype(bf16)
        for d in (2, 1, 3):
            ag_copy(slot, k, d).start()

    def finish(slot):
        for k in range(PIECES):
            for d in (1, 3, 2):
                ag_copy(slot, k, d).wait_recv()
        summed[slot] = gathered[slot]

    lax.fori_loop(0, IMAGES // 2 - 1, second_pass, 0)
    arrived(IMAGES - 2)
    add_grad(1, xs1, top, IMAGES - 2, 1)
    step_back(IMAGES - 2, 0)

    @pl.when(over_links)
    def _():
        add_grad(0, xs0, a1, IMAGES - 2, 1)

    arrived(IMAGES - 1)
    add_grad(1, xs1, top, IMAGES - 1, 1)
    scatter(1)
    step_back(IMAGES - 1, 1)

    @pl.when(over_links)
    def _():
        add_grad(0, xs0, a1, IMAGES - 1, 1)

    @pl.when(jnp.logical_not(over_links))
    def _():
        add_grad(0, xs0, a1, IMAGES - 4, 4)

    scatter(0)
    order = [(slot, k) for slot in (1, 0) for k in range(PIECES)]
    for slot, k in order:
        exchange(slot, k)
    for slot, k in order:
        gather(slot, k)
    finish(1)
    finish(0)

    for slot in range(2):
        for k in range(PIECES):
            for d in (1, 2, 3):
                rs_copy(slot, k, d).wait_send()
                ag_copy(slot, k, d).wait_send()
            z_copy(slot, k).wait_send()

    def drain(i, carry):
        @pl.when(has_below)
        def _():
            send_copy(i).wait_send()

        return carry

    lax.fori_loop(0, IMAGES, drain, 0)


def deliver(low_v, sum_v, low_out, grad_out, grad_v, low_sem, grad_sem):
    def low_copy(i):
        return pltpu.make_async_copy(low_v.at[i], low_out.at[i], low_sem.at[i])

    def grad_copy(slot):
        return pltpu.make_async_copy(grad_v.at[slot], grad_out.at[slot], grad_sem.at[slot])

    for i in range(IMAGES):
        low_copy(i).start()
    for slot in range(2):
        grad_v[slot] = sum_v[slot].astype(f32)
        grad_copy(slot).start()
    for slot in range(2):
        grad_copy(slot).wait()
    for i in range(IMAGES):
        low_copy(i).wait()


def body(u_c, lam_c, weights):
    image = (IMAGES, PAIRS, 2, W, C)
    pair = (IMAGES, PAIRS, W, 2 * C)
    patch = (PAIRS + 1, W, 2 * K)
    wide = (3, 2 * K, 2 * C)
    vmem, dma = pltpu.VMEM, pltpu.SemaphoreType.DMA
    low, grad = pl.pallas_call(
        kernel,
        out_shape=(pltpu.VMEM(image, bf16), pltpu.VMEM((2, 4, CHUNK, C), bf16)),
        in_specs=[pl.BlockSpec(memory_space=pl.ANY)] * 3,
        out_specs=(pl.BlockSpec(memory_space=vmem),) * 2,
        scratch_shapes=[
            vmem(image, bf16), vmem(image, bf16), vmem((2, 3, 3, C, C), bf16),
            vmem((IMAGES,) + patch, bf16), vmem((IMAGES,) + patch, bf16), vmem((2,) + patch, bf16), vmem(patch, bf16),
            vmem((2, PAIRS, W, 2 * C), bf16), vmem(pair, bf16),
            vmem(pair, bf16), vmem(pair, bf16), vmem(pair, bf16),
            vmem((2, 3, 2 * K, 2 * C), f32),
            vmem(wide, bf16), vmem(wide, bf16), vmem(wide, bf16),
            vmem((2, 9 * C, C), bf16), vmem((2, 3, CHUNK, C), bf16),
            vmem((2, CHUNK, C), bf16), vmem((2, CHUNK, C), bf16),
            vmem((2, 4, CHUNK, C), bf16),
            dma((IMAGES,)), dma((IMAGES,)), dma((2,)),
            dma((IMAGES,)), dma((IMAGES,)),
            dma((2, PIECES, 3)), dma((2, PIECES, 3)), dma((2, PIECES)), dma((2, PIECES)),
            dma((2, PIECES, 3)), dma((2, PIECES, 3)),
        ],
        compiler_params=pltpu.CompilerParams(
            collective_id=0, has_side_effects=True, vmem_limit_bytes=52 * 2**20
        ),
        cost_estimate=pl.CostEstimate(flops=15 * 10**9, bytes_accessed=10**7, transcendentals=2 * 10**6),
        name="relax",
    )(u_c.reshape(image), lam_c.reshape(image), weights)
    low, grad = pl.pallas_call(
        deliver,
        out_shape=(
            jax.ShapeDtypeStruct(image, bf16),
            jax.ShapeDtypeStruct((2, 4, CHUNK, C), f32),
        ),
        in_specs=[pl.BlockSpec(memory_space=vmem)] * 2,
        out_specs=(pl.BlockSpec(memory_space=pl.ANY),) * 2,
        scratch_shapes=[vmem((2, 4, CHUNK, C), f32), dma((IMAGES,)), dma((2,))],
        compiler_params=pltpu.CompilerParams(vmem_limit_bytes=8 * 2**20),
        name="deliver",
    )(low, grad)
    return low.reshape(1, IMAGES, 2 * PAIRS, W, C), grad.reshape(2, 3, 3, C, C)


def solution(mesh):
    placed = (
        P("layer", "batch", None, None, None),
        P("layer", "batch", None, None, None),
        P("layer", None, None, None, None),
    )
    return jax.shard_map(
        body,
        mesh=mesh,
        in_specs=placed,
        out_specs=(P("layer", "batch", None, None, None), P("layer", None, None, None, None)),
        check_vma=False,
    )
```

```python
import functools

import jax
import jax.numpy as jnp
from jax import lax
from jax.experimental import pallas as pl
from jax.experimental.pallas import tpu as pltpu
from jax.sharding import PartitionSpec as P

f32 = jnp.float32
bf16 = jnp.bfloat16
MESH = pl.DeviceIdType.MESH
IMAGES = 8
PAIRS = 16
ROWS = 8
CHUNKS = tuple(range(0, PAIRS, ROWS))
W = 32
C = 128
K = 3 * C
CHUNK = 288
PIECES = 3
PIECE = CHUNK // PIECES
TAPS = (((0, 0, 0), (0, 1, 1)), ((0, 1, 0), (1, 0, 1)), ((1, 0, 0), (1, 1, 1)))
depth_step = 0.5


def silu_parts(v):
    t = 0.5 * jnp.tanh(0.5 * v) + 0.5
    return v * t, depth_step * (t * (1.0 + v * (1.0 - t)))


def put_rows(x_ref, at, parity, value):
    column = lax.broadcasted_iota(jnp.int32, value.shape, 1)
    before = jnp.where(column == 0, 0.0, pltpu.roll(value, 1, 1))
    after = jnp.where(column == W - 1, 0.0, pltpu.roll(value, W - 1, 1))
    first = at if parity == 0 else at + 1
    lane = K if parity == 0 else 0
    for b, part in enumerate((before, value, after)):
        x_ref[first : first + ROWS, :, lane + b * C : lane + (b + 1) * C] = part.astype(bf16)


def clear_edges(x_ref):
    x_ref[0, :, 0:K] = jnp.zeros((W, K), bf16)
    x_ref[PAIRS, :, K : 2 * K] = jnp.zeros((W, K), bf16)


def conv(x_ref, w_ref, at):
    n = ROWS // 2 * W
    d = x_ref[at : at + ROWS].reshape(ROWS // 2, 2, W, 2 * K)
    later = x_ref[at + 1 : at + ROWS + 1].reshape(ROWS // 2, 2, W, 2 * K)
    d0, d1, d2 = (v.reshape(n, 2 * K) for v in (d[:, 0], d[:, 1], later[:, 1]))
    shared = jnp.dot(d1, w_ref[1], preferred_element_type=f32)
    upper = shared + jnp.dot(d0 - d1, w_ref[0], preferred_element_type=f32)
    lower = shared + jnp.dot(d2 - d1, w_ref[2], preferred_element_type=f32)
    shape = (ROWS // 2, W, 2 * C)
    y = jnp.stack([upper.reshape(shape), lower.reshape(shape)], axis=1).reshape(ROWS, W, 2 * C)
    return y[:, :, :C], y[:, :, C:]


def fill_weights(dst, src, layer, transposed):
    for t in range(2):
        for q in range(2):
            for p in range(2):
                a = 2 * t + q - p
                for b in range(3):
                    rows = slice(q * K + b * C, q * K + (b + 1) * C)
                    cols = slice(p * C, (p + 1) * C)
                    if not 0 <= a <= 2:
                        dst[2 * t, rows, cols] = jnp.zeros((C, C), bf16)
                    elif transposed:
                        dst[2 * t, rows, cols] = src[layer, 2 - a, 2 - b].T
                    else:
                        dst[2 * t, rows, cols] = src[layer, a, b]
    dst[1] = dst[0] + dst[2]


def kernel(
    u_hbm, lam_hbm, w_hbm, low_v, summed,
    u_v, lam_v, w_v, xs0, xs1, xq, xr, g0, g1, bottom, top, a1, acc,
    wf, wt0, wt1, part, rs_buf, z_own, z_buf, gathered,
    u_sem, lam_sem, w_sem, send_sem, recv_sem,
    rs_send, rs_recv, z_send, z_recv, ag_send, ag_recv,
):
    layer = lax.axis_index("layer")
    batch = lax.axis_index("batch")
    x, zh = batch // 2, batch % 2
    below, above = jnp.maximum(layer - 1, 0), jnp.minimum(layer + 1, 31)
    has_below, has_above = layer > 0, layer < 31
    over_links = layer % 2 == 1

    def at_x(d):
        return (layer, ((x + d) % 4) * 2 + zh)

    twin = (layer, x * 2 + 1 - zh)

    def w_copy(slot):
        return pltpu.make_async_copy(w_hbm.at[slot], w_v.at[slot], w_sem.at[slot])

    def u_copy(i):
        return pltpu.make_async_copy(u_hbm.at[i], u_v.at[i], u_sem.at[i])

    def lam_copy(i):
        return pltpu.make_async_copy(lam_hbm.at[i], lam_v.at[i], lam_sem.at[i])

    u_copy(0).start()
    w_copy(0).start()
    lam_copy(0).start()
    w_copy(1).start()
    barrier = pltpu.get_barrier_semaphore()

    @pl.when(has_below)
    def _():
        pl.semaphore_signal(barrier, inc=1, device_id=(below, batch), device_id_type=MESH)

    @pl.when(has_above)
    def _():
        pl.semaphore_signal(barrier, inc=1, device_id=(above, batch), device_id_type=MESH)

    for d in (1, 2, 3):
        pl.semaphore_signal(barrier, inc=1, device_id=at_x(d), device_id_type=MESH)
    pl.semaphore_signal(barrier, inc=1, device_id=twin, device_id_type=MESH)

    clear_edges(xq.at[0])
    clear_edges(xq.at[1])
    clear_edges(xr)
    acc[...] = jnp.zeros_like(acc)

    def clear(i, carry):
        clear_edges(xs0.at[i])
        clear_edges(xs1.at[i])
        return carry

    lax.fori_loop(0, IMAGES, clear, 0)
    def send_copy(i):
        return pltpu.make_async_remote_copy(
            src_ref=bottom.at[i], dst_ref=top.at[i], send_sem=send_sem.at[i], recv_sem=recv_sem.at[i],
            device_id=(below, batch), device_id_type=MESH,
        )

    def lanes(p):
        return slice(p * C, (p + 1) * C)

    def load(i):
        u_copy(i).wait()
        lam_copy(i).wait()

    def open_state(i, slot, at):
        rows = slice(at, at + ROWS)
        for p in range(2):
            s, g = silu_parts(u_v[i, rows, p].astype(f32))
            put_rows(xs0.at[i], at, p, s)
            g0[slot, rows, :, lanes(p)] = g.astype(bf16)

    def open_adjoint(i, slot, at):
        for p in range(2):
            put_rows(xq.at[slot], at, p, lam_v[i, at : at + ROWS, p].astype(f32))

    def first_pass(i, carry):
        now, then = lax.rem(i, 2), lax.rem(i + 1, 2)
        ahead = jnp.minimum(i + 1, IMAGES - 1)

        @pl.when(i < IMAGES - 1)
        def _():
            load(ahead)

        for at in CHUNKS:
            rows = slice(at, at + ROWS)
            for p, y in enumerate(conv(xs0.at[i], wf, at)):
                moved = (u_v[i, rows, p].astype(f32) + depth_step * y).astype(bf16).astype(f32)
                s, g = silu_parts(moved)
                put_rows(xs1.at[i], at, p, s)
                g1[i, rows, :, lanes(p)] = g.astype(bf16)
        for at in CHUNKS:
            rows = slice(at, at + ROWS)
            for p, y in enumerate(conv(xq.at[now], wt1, at)):
                g = g1[i, rows, :, lanes(p)].astype(f32)
                put_rows(xr, at, p, (lam_v[i, rows, p].astype(f32) + g * y).astype(bf16).astype(f32))
            open_adjoint(ahead, then, at)
        for at in CHUNKS:
            rows = slice(at, at + ROWS)
            for p, y in enumerate(conv(xr, wt0, at)):
                first, lane = (at, K + C) if p == 0 else (at + 1, C)
                centre = xr[first : first + ROWS, :, lane : lane + C].astype(f32)
                g = g0[now, rows, :, lanes(p)].astype(f32)
                bottom[i, rows, :, lanes(p)] = (centre + g * y).astype(bf16)
            open_state(ahead, then, at)

        @pl.when(has_below)
        def _():
            send_copy(i).start()

        @pl.when(jnp.logical_not(has_above))
        def _():
            for p in range(2):
                top[i, :, :, lanes(p)] = lam_v[i, :, p]

        return carry

    u_copy(0).wait()
    for at in CHUNKS:
        open_state(0, 0, at)
    lam_copy(0).wait()
    w_copy(0).wait()
    w_copy(1).wait()
    for i in range(1, IMAGES):
        u_copy(i).start()
        lam_copy(i).start()
    fill_weights(wf, w_v, 0, False)
    for at in CHUNKS:
        open_adjoint(0, 0, at)
    fill_weights(wt1, w_v, 1, True)
    fill_weights(wt0, w_v, 0, True)
    peers = 4 + jnp.where(has_below, 1, 0) + jnp.where(has_above, 1, 0)
    pl.semaphore_wait(barrier, peers)

    lax.fori_loop(0, IMAGES, first_pass, 0)

    def add_grad(slot, xs, adj, i, count):
        n = count * PAIRS // 2 * W
        r = adj[pl.ds(i, count)].reshape(count, PAIRS // 2, 2, W, 2 * C)
        d = xs[pl.ds(i, count), 0:PAIRS].reshape(count, PAIRS // 2, 2, W, 2 * K)
        later = xs[pl.ds(i, count), 1 : PAIRS + 1].reshape(count, PAIRS // 2, 2, W, 2 * K)
        r0, r1 = r[:, :, 0], r[:, :, 1]
        d0, d1, d2 = d[:, :, 0], d[:, :, 1], later[:, :, 1]
        for t, (left, right) in enumerate(((d0 - d1, r0), (d1, r0 + r1), (d2 - d1, r1))):
            acc[slot, t] += lax.dot_general(
                left.reshape(n, 2 * K), right.reshape(n, 2 * C),
                (((0,), (0,)), ((), ())), preferred_element_type=f32,
            )

    def step_back(i, slot):
        for at in CHUNKS:
            rows = slice(at, at + ROWS)
            for p in range(2):
                put_rows(xq.at[slot], at, p, top[i, rows, :, lanes(p)].astype(f32))
        for at in CHUNKS:
            rows = slice(at, at + ROWS)
            for p, y in enumerate(conv(xq.at[slot], wt1, at)):
                moved = top[i, rows, :, lanes(p)].astype(f32) + g1[i, rows, :, lanes(p)].astype(f32) * y
                a1[i, rows, :, lanes(p)] = moved.astype(bf16)
                low_v[i, rows, p] = moved.astype(bf16)

    def arrived(i):
        @pl.when(has_above)
        def _():
            send_copy(i).wait_recv()

    def second_pass(j, carry):
        for slot in range(2):
            arrived(2 * j + slot)
            step_back(2 * j + slot, slot)
        add_grad(1, xs1, top, 2 * j, 2)

        @pl.when(over_links)
        def _():
            add_grad(0, xs0, a1, 2 * j, 2)

        return carry

    factor = depth_step / (IMAGES * 8)

    def piece(k, first=0):
        return pl.ds(pl.multiple_of(first + k * PIECE, 16), PIECE)

    def rs_copy(slot, k, d):
        to = (x + d) % 4
        return pltpu.make_async_remote_copy(
            src_ref=part.at[slot, piece(k, to * CHUNK)], dst_ref=rs_buf.at[slot, d - 1, piece(k)],
            send_sem=rs_send.at[slot, k, d - 1], recv_sem=rs_recv.at[slot, k, d - 1],
            device_id=at_x(d), device_id_type=MESH,
        )

    def z_copy(slot, k):
        return pltpu.make_async_remote_copy(
            src_ref=z_own.at[slot, piece(k)], dst_ref=z_buf.at[slot, piece(k)],
            send_sem=z_send.at[slot, k], recv_sem=z_recv.at[slot, k],
            device_id=twin, device_id_type=MESH,
        )

    def ag_copy(slot, k, d):
        return pltpu.make_async_remote_copy(
            src_ref=gathered.at[slot, x, piece(k)], dst_ref=gathered.at[slot, x, piece(k)],
            send_sem=ag_send.at[slot, k, d - 1], recv_sem=ag_recv.at[slot, k, d - 1],
            device_id=at_x(d), device_id_type=MESH,
        )

    def scatter(slot):
        for a, terms in enumerate(TAPS):
            total = 0.0
            for t, q, p in terms:
                block = (slice(q * K, (q + 1) * K), lanes(p))
                total += acc[slot, t, *block] + acc[slot, t + 1, *block]
            part[slot, a * K : (a + 1) * K] = (factor * total).astype(bf16)
        for k in range(PIECES):
            for d in (2, 1, 3):
                rs_copy(slot, k, d).start()

    def exchange(slot, k):
        for d in (1, 3, 2):
            rs_copy(slot, k, d).wait_recv()
        total = part[slot, piece(k, x * CHUNK)].astype(f32)
        for d in (1, 2, 3):
            total += rs_buf[slot, d - 1, piece(k)].astype(f32)
        z_own[slot, piece(k)] = total.astype(bf16)
        z_copy(slot, k).start()

    def gather(slot, k):
        z_copy(slot, k).wait_recv()
        total = z_own[slot, piece(k)].astype(f32) + z_buf[slot, piece(k)].astype(f32)
        gathered[slot, x, piece(k)] = total.astype(bf16)
        for d in (2, 1, 3):
            ag_copy(slot, k, d).start()

    def finish(slot):
        for k in range(PIECES):
            for d in (1, 3, 2):
                ag_copy(slot, k, d).wait_recv()
        summed[slot] = gathered[slot]

    lax.fori_loop(0, IMAGES // 2 - 1, second_pass, 0)
    arrived(IMAGES - 2)
    add_grad(1, xs1, top, IMAGES - 2, 1)
    step_back(IMAGES - 2, 0)

    @pl.when(over_links)
    def _():
        add_grad(0, xs0, a1, IMAGES - 2, 1)

    arrived(IMAGES - 1)
    add_grad(1, xs1, top, IMAGES - 1, 1)
    scatter(1)
    step_back(IMAGES - 1, 1)

    @pl.when(over_links)
    def _():
        add_grad(0, xs0, a1, IMAGES - 1, 1)

    @pl.when(jnp.logical_not(over_links))
    def _():
        add_grad(0, xs0, a1, 0, 4)
        add_grad(0, xs0, a1, IMAGES - 4, 4)

    scatter(0)
    order = [(slot, k) for slot in (1, 0) for k in range(PIECES)]
    for slot, k in order:
        exchange(slot, k)
    for slot, k in order:
        gather(slot, k)
    finish(1)
    finish(0)

    for slot in range(2):
        for k in range(PIECES):
            for d in (1, 2, 3):
                rs_copy(slot, k, d).wait_send()
                ag_copy(slot, k, d).wait_send()
            z_copy(slot, k).wait_send()

    def drain(i, carry):
        @pl.when(has_below)
        def _():
            send_copy(i).wait_send()

        return carry

    lax.fori_loop(0, IMAGES, drain, 0)


def deliver(low_v, sum_v, low_out, grad_out, grad_v, low_sem, grad_sem):
    def low_copy(i):
        return pltpu.make_async_copy(low_v.at[i], low_out.at[i], low_sem.at[i])

    def grad_copy(slot):
        return pltpu.make_async_copy(grad_v.at[slot], grad_out.at[slot], grad_sem.at[slot])

    for i in range(IMAGES):
        low_copy(i).start()
    for slot in range(2):
        grad_v[slot] = sum_v[slot].astype(f32)
        grad_copy(slot).start()
    for slot in range(2):
        grad_copy(slot).wait()
    for i in range(IMAGES):
        low_copy(i).wait()


def body(u_c, lam_c, weights):
    image = (IMAGES, PAIRS, 2, W, C)
    pair = (IMAGES, PAIRS, W, 2 * C)
    patch = (PAIRS + 1, W, 2 * K)
    wide = (3, 2 * K, 2 * C)
    vmem, dma = pltpu.VMEM, pltpu.SemaphoreType.DMA
    low, grad = pl.pallas_call(
        kernel,
        out_shape=(pltpu.VMEM(image, bf16), pltpu.VMEM((2, 4, CHUNK, C), bf16)),
        in_specs=[pl.BlockSpec(memory_space=pl.ANY)] * 3,
        out_specs=(pl.BlockSpec(memory_space=vmem),) * 2,
        scratch_shapes=[
            vmem(image, bf16), vmem(image, bf16), vmem((2, 3, 3, C, C), bf16),
            vmem((IMAGES,) + patch, bf16), vmem((IMAGES,) + patch, bf16), vmem((2,) + patch, bf16), vmem(patch, bf16),
            vmem((2, PAIRS, W, 2 * C), bf16), vmem(pair, bf16),
            vmem(pair, bf16), vmem(pair, bf16), vmem(pair, bf16),
            vmem((2, 3, 2 * K, 2 * C), f32),
            vmem(wide, bf16), vmem(wide, bf16), vmem(wide, bf16),
            vmem((2, 9 * C, C), bf16), vmem((2, 3, CHUNK, C), bf16),
            vmem((2, CHUNK, C), bf16), vmem((2, CHUNK, C), bf16),
            vmem((2, 4, CHUNK, C), bf16),
            dma((IMAGES,)), dma((IMAGES,)), dma((2,)),
            dma((IMAGES,)), dma((IMAGES,)),
            dma((2, PIECES, 3)), dma((2, PIECES, 3)), dma((2, PIECES)), dma((2, PIECES)),
            dma((2, PIECES, 3)), dma((2, PIECES, 3)),
        ],
        compiler_params=pltpu.CompilerParams(
            collective_id=0, has_side_effects=True, vmem_limit_bytes=52 * 2**20
        ),
        cost_estimate=pl.CostEstimate(flops=15 * 10**9, bytes_accessed=10**7, transcendentals=2 * 10**6),
        name="relax",
    )(u_c.reshape(image), lam_c.reshape(image), weights)
    low, grad = pl.pallas_call(
        deliver,
        out_shape=(
            jax.ShapeDtypeStruct(image, bf16),
            jax.ShapeDtypeStruct((2, 4, CHUNK, C), f32),
        ),
        in_specs=[pl.BlockSpec(memory_space=vmem)] * 2,
        out_specs=(pl.BlockSpec(memory_space=pl.ANY),) * 2,
        scratch_shapes=[vmem((2, 4, CHUNK, C), f32), dma((IMAGES,)), dma((2,))],
        compiler_params=pltpu.CompilerParams(vmem_limit_bytes=8 * 2**20),
        name="deliver",
    )(low, grad)
    return low.reshape(1, IMAGES, 2 * PAIRS, W, C), grad.reshape(2, 3, 3, C, C)


def solution(mesh):
    placed = (
        P("layer", "batch", None, None, None),
        P("layer", "batch", None, None, None),
        P("layer", None, None, None, None),
    )
    return jax.shard_map(
        body,
        mesh=mesh,
        in_specs=placed,
        out_specs=(P("layer", "batch", None, None, None), P("layer", None, None, None, None)),
        check_vma=False,
    )
```
